32 devices in a mesh: beam: 2 (over y), bin: 4 (over z), chan: 4 (over x, core).
Axes of the slice: x: 2, y: 2, z: 4, core: 2. Of those that a mesh axis runs over, the one named last changes fastest.
Arguments:
- spectra: bfloat16 [2, 8192, 1024], P(None, ('beam', 'chan', 'bin')), parts along dimension 1, may hold values from -6 to 6
- dm_trials: int32 [64], replicated, may hold values from 0 to 1023
- chan_delay: int32 [4096], replicated, may hold values from 0 to 32767
- template_bank: bfloat16 [2, 256, 256], replicated, may hold values from -0.25 to 0.25
- template_ids: int32 [128], replicated, may hold values from 0 to 255
Outputs:
- powers: bfloat16 [128, 128, 1024], P(('beam', 'chan'), None, 'bin'), parts along dimension 0
The draws below stay inside these ranges and needn't reach their ends.
There are 2 independent parts, one for each index of `beam`. The reference program is written for one: setup_inputs(seed, part) draws one part's arguments, and reference() takes and returns one part's arrays. A program takes and returns all parts, laid end to end along the dimension named above; an argument that names none is the same for every part. Nothing has to cross between parts.
All inputs are finite; a program needn't handle non-finite values.
Results may differ from the reference program's by a relative error of at most 0.0095.
Values may be sent and summed in bfloat16 or wider, within the bound.
No kernel may reach another device: no remote copies, remote signals or barrier semaphores. Data moves between devices by JAX's collectives and lax.ppermute only.
A program may use at most 64 MiB of HBM per device.

```python
import math
import jax
import jax.numpy as jnp
from jax import lax

CHANS = 4096
TRIALS = 64
TEMPLATES = 128
BANK = 256
EDGE = 128
TAPS = 256
BINS = 1024


def touch_ends(drawn, key, smallest, largest):
    longest = drawn.shape.index(max(drawn.shape))
    spots = []
    for shift in (0, 1):
        where = [jax.random.randint(jax.random.fold_in(key, axis), (), 0, length) for axis, length in enumerate(drawn.shape)]
        where[longest] = (where[longest] + shift) % drawn.shape[longest]
        spots.append(tuple(where))
    return drawn.at[spots[0]].set(smallest).at[spots[1]].set(largest)


def shard_levels(rng, shape, cuts, low, largest):
    def one(dim, parts):
        draws = jax.random.uniform(jax.random.fold_in(jax.random.fold_in(rng, 6), dim), (parts,), jnp.float32, low / len(cuts), largest / len(cuts))
        return jnp.repeat(jnp.exp(draws), shape[dim] // parts).reshape((-1,) + (1,) * (len(shape) - dim - 1))

    level = one(*cuts[0])
    for cut in cuts[1:]:
        level = level * one(*cut)
    return level


def gaussian(stream_key, extent, width, bound, shards=(), kind=jnp.bfloat16):
    result = jax.random.normal(stream_key, extent, jnp.float32) * width
    if len(shards) > 0:
        result = shard_levels(stream_key, extent, shards, -0.22, 0.18) * result
    return jnp.clip(result, min=-bound, max=bound).astype(kind)


def setup_inputs(seed: int = 0, part: int = 0) -> dict:
    key_of = jax.random.split(jax.random.key(seed), 6)
    part_splits = jax.random.split(jax.random.fold_in(key_of[5], part), 6)
    return {
        "spectra": gaussian(part_splits[0], (2, CHANS, BINS), 1.0, 6.0, ((1, 16),)),
        "dm_trials": touch_ends(jax.random.randint(key_of[1], (TRIALS,), 0, 1024), jax.random.fold_in(key_of[1], 1), 0, 1023).astype(jnp.int32),
        "chan_delay": touch_ends(jax.random.randint(key_of[2], (CHANS,), 0, 32768), jax.random.fold_in(key_of[2], 1), 0, 32767).astype(jnp.int32),
        "template_bank": gaussian(key_of[3], (2, BANK, TAPS), (2 * TAPS) ** -0.5, 0.25),
        "template_ids": touch_ends(jax.random.randint(key_of[4], (TEMPLATES,), 0, BANK), jax.random.fold_in(key_of[4], 1), 0, BANK - 1).astype(jnp.int32),
    }


def reference(spectra, dm_trials, chan_delay, template_bank, template_ids):
    samples = 2 * BINS
    block_size = math.gcd(BINS, 32)
    delays = dm_trials[:, None] * chan_delay[None, :] % samples
    starts_list = jnp.arange(BINS // block_size, dtype=jnp.int32) * block_size

    def one_block(first_bin):
        spec_part = lax.dynamic_slice_in_dim(spectra, first_bin, block_size, 2).astype(jnp.float32)
        bin_ids = first_bin + jnp.arange(block_size, dtype=jnp.int32)
        turn_counts = bin_ids[:, None, None] * delays[None, :, :] % samples
        angles = turn_counts.astype(jnp.float32) * (2.0 * math.pi / samples)
        cos_half = lax.optimization_barrier(jnp.cos(angles).astype(jnp.bfloat16))
        sin_half = lax.optimization_barrier((-jnp.sin(angles)).astype(jnp.bfloat16))
        cosine = cos_half.astype(jnp.float32)
        sine_part = sin_half.astype(jnp.float32)
        real_part = jnp.einsum('fdc,cf->df', cosine, spec_part[0]) - jnp.einsum('fdc,cf->df', sine_part, spec_part[1])
        imag_part = jnp.einsum('fdc,cf->df', cosine, spec_part[1]) + jnp.einsum('fdc,cf->df', sine_part, spec_part[0])
        return jnp.stack([real_part, imag_part], 1)
    pieces = lax.map(one_block, starts_list)
    summed = pieces.transpose(1, 2, 0, 3).reshape(TRIALS, 2, BINS)
    dedispersed = (summed * (1.0 / math.sqrt(CHANS))).astype(jnp.bfloat16)
    templates = jnp.take(template_bank, template_ids, axis=1).astype(jnp.float32)
    length = BINS + TAPS
    signal_rows = dedispersed.astype(jnp.float32)
    signal_rows = signal_rows[:, 0] + 1j * signal_rows[:, 1]
    signal_rows = jnp.pad(signal_rows, ((0, 0), (EDGE, length - BINS - EDGE)))
    tap_rows = templates[0] + 1j * templates[1]
    flipped_taps = jnp.concatenate([tap_rows[:, :1], jnp.zeros((TEMPLATES, length - TAPS), tap_rows.dtype), tap_rows[:, :0:-1]], 1)
    tap_freq = jnp.fft.fft(flipped_taps, axis=1)

    def one_trial(signal):
        response = jnp.fft.ifft(jnp.fft.fft(signal)[None, :] * tap_freq, axis=1)[:, :BINS]
        real_resp = jnp.real(response)
        imag_resp = jnp.imag(response)
        return (real_resp * real_resp + imag_resp * imag_resp).astype(jnp.bfloat16)
    return lax.map(one_trial, signal_rows)
```

```python
import functools
import math

import jax
import jax.numpy as jnp
from jax import lax
from jax.experimental import pallas as pl
from jax.experimental.pallas import tpu as pltpu
from jax.sharding import PartitionSpec as P

EDGE = 128
LANES = 128
SUB = 8
F32 = jnp.float32
BF16 = jnp.bfloat16


def sincos(turn, samples):
    quarter = samples // 4
    quadrant = (turn + quarter // 2) // quarter if quarter & (quarter - 1) else lax.shift_right_logical(
        turn + quarter // 2, jnp.full_like(turn, quarter.bit_length() - 1)
    )
    y = (turn - quadrant * quarter).astype(F32) * (2.0 * math.pi / samples)
    z = y * y
    s = y + y * z * (-1.6666654611e-1 + z * (8.3321608736e-3 - z * 1.9515295891e-4))
    c = 1.0 - 0.5 * z + z * z * (4.166664568298827e-2 + z * (-1.388731625493765e-3 + z * 2.443315711809948e-5))
    odd = (quadrant & 1) == 1
    cos_abs = jnp.where(odd, s, c)
    sin_abs = jnp.where(odd, c, s)
    cos = jnp.where(((quadrant + 1) & 2) == 2, -cos_abs, cos_abs)
    sin = jnp.where((quadrant & 2) == 2, -sin_abs, sin_abs)
    return cos, sin


def dedisperse_kernel(trials_each, bins, dm_ref, cd_ref, sp_ref, send_ref, keep_ref, ph, cdcol, y, xs, dms):
    step = pl.program_id(0)
    channels, tile = sp_ref.shape[1], sp_ref.shape[2]
    samples = 2 * bins
    half = LANES // 2
    chunks = bins // half
    chan = lax.axis_index("chan")
    block = chan * lax.axis_size("bin") + lax.axis_index("bin")

    @pl.when(step == 0)
    def _():
        if channels >= LANES:
            for k in range(channels // LANES):
                row = cd_ref[pl.ds(block * (channels // LANES) + k, 1), :]
                cdcol[pl.ds(k * LANES, LANES), :] = jnp.broadcast_to(row, (LANES, LANES)).T
            cd = cdcol[...]
        else:
            first = block * channels
            row = cd_ref[pl.ds(first // LANES, 1), :]
            cdcol[...] = jnp.broadcast_to(row, (LANES, LANES)).T
            cd = cdcol[pl.ds(pl.multiple_of(first % LANES, SUB), channels), :]
        lane = lax.broadcasted_iota(jnp.int32, cd.shape, 1)
        turn = (lane & (half - 1)) * cd - jnp.where(lane >= half, samples // 4, 0)
        u, v = sincos(turn & (samples - 1), samples)
        du, dv = sincos((half * cd) & (samples - 1), samples)
        for j in range(chunks):
            value = u
            if j == 0:
                value = jnp.where(lane == half, (1 - 2 * (cd & 1)).astype(F32), u)
            ph[:, j * LANES : (j + 1) * LANES] = value.astype(BF16)
            u, v = u * du - v * dv, v * du + u * dv
        where = lax.broadcasted_iota(jnp.int32, (SUB, LANES), 1)
        trial = ((where // (2 * trials_each)) ^ chan) * trials_each + (where & (trials_each - 1))
        dm = jnp.concatenate([dm_ref[...], dm_ref[...]], axis=1)
        dms[...] = jnp.take_along_axis(jnp.broadcast_to(dm, (SUB, LANES)), trial, axis=1)
        edge = jnp.zeros((send_ref.shape[0], EDGE), BF16)
        for ref in (send_ref, keep_ref):
            ref[:, :EDGE] = edge
            ref[:, bins + EDGE :] = edge

    lhs = jnp.concatenate([sp_ref[0], sp_ref[1]], axis=1)
    y[...] = lax.dot_general(lhs, ph[...], (((0,), (0,)), ((), ())), preferred_element_type=F32)
    dm = dms[...]
    lane = lax.broadcasted_iota(jnp.int32, (SUB, LANES), 1)
    row = lax.broadcasted_iota(jnp.int32, (SUB, LANES), 0)
    imag = (lane & trials_each) != 0

    def gather(group, _):
        base = pl.multiple_of(group * SUB, SUB)
        g = ((step * tile + base + row) * dm) & (samples - 1)
        upper = g > bins
        near = jnp.where(upper, samples - g, g)
        chunk = lax.shift_right_logical(near, jnp.full_like(near, half.bit_length() - 1)) & (chunks - 1)
        swap = imag != (g == bins)
        low = near & (half - 1)
        at_re = low + jnp.where(swap, half, 0)
        at_im = at_re ^ half
        from_re = from_im = jnp.zeros((SUB, LANES), F32)
        for j in range(chunks):
            here = chunk == j
            columns = slice(j * LANES, (j + 1) * LANES)
            got = jnp.take_along_axis(y[pl.ds(base, SUB), columns], at_re, axis=1)
            from_re = jnp.where(here, got, from_re)
            got = jnp.take_along_axis(y[pl.ds(tile + base, SUB), columns], at_im, axis=1)
            from_im = jnp.where(here, got, from_im)
        sign = jnp.where((g & (bins - 1)) == 0, 0.0, jnp.where(upper, -1.0, 1.0))
        re_weight = jnp.where(imag, -sign, 1.0)
        im_weight = jnp.where(imag, 1.0, sign)
        xs[pl.ds(base, SUB), :] = from_re * re_weight + from_im * im_weight
        return 0

    lax.fori_loop(0, tile // SUB, gather, 0)
    out = xs[...].T.astype(BF16)
    columns = pl.ds(pl.multiple_of(EDGE + step * tile, LANES), tile)
    wide = 2 * trials_each
    for k in range(LANES // wide):
        ref = (keep_ref, send_ref)[k % 2]
        ref[(k // 2) * wide : (k // 2 + 1) * wide, columns] = out[k * wide : (k + 1) * wide]


def dedisperse(spectra, dm_trials, chan_delay, trials_each):
    _, channels, bins = spectra.shape
    tile = LANES
    rows = LANES // 2
    whole = lambda shape: pl.BlockSpec(shape, lambda i: (0,) * len(shape))
    delays = chan_delay.reshape(-1, LANES)
    shape = jax.ShapeDtypeStruct((rows, bins + 2 * EDGE), BF16)
    return pl.pallas_call(
        functools.partial(dedisperse_kernel, trials_each, bins),
        grid=(bins // tile,),
        in_specs=[
            whole((1, dm_trials.shape[0])),
            whole(delays.shape),
            pl.BlockSpec((2, channels, tile), lambda i: (0, 0, i)),
        ],
        out_specs=[whole(shape.shape)] * 2,
        out_shape=[shape] * 2,
        scratch_shapes=[
            pltpu.VMEM((channels, 2 * bins), BF16),
            pltpu.VMEM((max(channels, LANES), LANES), jnp.int32),
            pltpu.VMEM((2 * tile, 2 * bins), F32),
            pltpu.VMEM((tile, LANES), F32),
            pltpu.VMEM((SUB, LANES), jnp.int32),
        ],
        compiler_params=pltpu.CompilerParams(vmem_limit_bytes=48 * 2**20),
        name="dedisperse",
    )(dm_trials.reshape(1, -1), delays, spectra)


def pick_kernel(bank_ref, ids_ref, out_ref):
    bank, taps = bank_ref.shape[1:]
    count = ids_ref.shape[1]
    rows = lax.broadcasted_iota(jnp.int32, (bank, count), 0)
    one_hot = jnp.where(rows == ids_ref[...], 1.0, 0.0).astype(BF16)
    at = lax.broadcasted_iota(jnp.int32, (taps, taps), 0)
    to = lax.broadcasted_iota(jnp.int32, (taps, taps), 1)
    flip = jnp.where(at == (to ^ 15), 1.0, 0.0).astype(BF16)
    chosen = []
    for part in range(2):
        taken = lax.dot_general(one_hot, bank_ref[part], (((0,), (0,)), ((), ())), preferred_element_type=F32)
        chosen.append(jnp.dot(taken.astype(BF16), flip, preferred_element_type=F32))
    re, im = chosen
    out_ref[:count, :taps] = re.astype(BF16)
    out_ref[:count, taps:] = (-im).astype(BF16)
    out_ref[count:, :taps] = im.astype(BF16)
    out_ref[count:, taps:] = re.astype(BF16)


def pick_templates(template_bank, template_ids):
    _, bank, taps = template_bank.shape
    count = template_ids.shape[0]
    return pl.pallas_call(
        pick_kernel,
        out_shape=jax.ShapeDtypeStruct((2 * count, 2 * taps), BF16),
        cost_estimate=pl.CostEstimate(flops=4 * count * bank * taps, bytes_accessed=2**20, transcendentals=0),
        name="pick_templates",
    )(template_bank, template_ids.reshape(1, -1))


def search_kernel(scale, taps, near_ref, far_ref, templates_ref, out_ref, signal, hankel):
    step = pl.program_id(0)
    each, count, bins = out_ref.shape
    rows, width = near_ref.shape
    trials = rows // 2

    @pl.when(step == 0)
    def _():
        total = near_ref[...].astype(F32) + far_ref[...].astype(F32)
        signal[...] = (total * scale).astype(BF16).astype(F32)

    for k in range(each):
        trial = step * each + k
        for part in range(2):
            line = signal[pl.ds(part * trials + trial, 1), :]
            skew = pltpu.roll(jnp.broadcast_to(line, (16, width)), width - 15, 1, stride=1, stride_axis=0)
            for e in range(LANES // 16):
                moved = skew if e == 0 else pltpu.roll(skew, width - 16 * e, 1)
                moved = moved.astype(BF16)
                for h in range(taps // LANES):
                    at = part * taps + h * LANES + 16 * e
                    hankel[k, at : at + 16, :] = moved[:, h * LANES : h * LANES + bins]
        response = jnp.dot(templates_ref[...], hankel[k], preferred_element_type=F32)
        re, im = response[:count], response[count:]
        out_ref[k] = (re * re + im * im).astype(BF16)


def search(near, far, templates, scale, bins):
    rows, width = near.shape
    trials = rows // 2
    taps = templates.shape[1] // 2
    count = templates.shape[0] // 2
    each = min(trials, 4)
    whole = lambda shape: pl.BlockSpec(shape, lambda i: (0,) * len(shape))
    return pl.pallas_call(
        functools.partial(search_kernel, scale, taps),
        grid=(trials // each,),
        in_specs=[whole(near.shape), whole(far.shape), whole(templates.shape)],
        out_specs=pl.BlockSpec((each, count, bins), lambda i: (i, 0, 0)),
        out_shape=jax.ShapeDtypeStruct((trials, count, bins), BF16),
        scratch_shapes=[pltpu.VMEM((rows, width), F32), pltpu.VMEM((each, 2 * taps, bins), BF16)],
        compiler_params=pltpu.CompilerParams(vmem_limit_bytes=48 * 2**20),
        name="search",
    )(near, far, templates)


def swap(cells, axis, distance):
    return lax.ppermute(cells, axis, [(i, i ^ distance) for i in range(lax.axis_size(axis))])


def local(spectra, dm_trials, chan_delay, template_bank, template_ids):
    owners, spans = lax.axis_size("chan"), lax.axis_size("bin")
    bins = spectra.shape[2]
    own_bins = bins // spans
    trials_each = dm_trials.shape[0] // owners
    scale = 1.0 / math.sqrt(chan_delay.shape[0])
    wide = 2 * trials_each
    templates = pick_templates(template_bank, template_ids)
    send, keep = dedisperse(spectra, dm_trials, chan_delay, trials_each)
    distance = 1
    while True:
        got = swap(send, "chan", distance)
        distance *= 2
        if distance == owners:
            break
        total = (keep.astype(F32) + got.astype(F32)).astype(BF16).reshape(-1, 2, wide, keep.shape[1])
        keep, send = total[:, 0].reshape(-1, keep.shape[1]), total[:, 1].reshape(-1, keep.shape[1])
    place = lax.axis_index("bin")
    part = spans // 2
    while part:
        total = (keep.astype(F32) + got.astype(F32)).astype(BF16)
        left, right = total[:, : part * own_bins + 2 * EDGE], total[:, part * own_bins :]
        upper = (place & part) != 0
        keep, send = jnp.where(upper, right, left), jnp.where(upper, left, right)
        got = swap(send, "bin", part)
        part //= 2
    return search(keep, got, templates, scale, own_bins)


def solution(mesh):
    in_specs = (P(None, ("beam", "chan", "bin"), None), P(), P(), P(), P())
    out_specs = P(("beam", "chan"), None, "bin")
    return jax.shard_map(local, mesh=mesh, in_specs=in_specs, out_specs=out_specs, check_vma=False)
```

```python
import functools
import math

import jax
import jax.numpy as jnp
from jax import lax
from jax.experimental import pallas as pl
from jax.experimental.pallas import tpu as pltpu
from jax.sharding import PartitionSpec as P

EDGE = 128
LANES = 128
SUB = 8
F32 = jnp.float32
BF16 = jnp.bfloat16


def sincos(turn, samples):
    quarter = samples // 4
    quadrant = (turn + quarter // 2) // quarter if quarter & (quarter - 1) else lax.shift_right_logical(
        turn + quarter // 2, jnp.full_like(turn, quarter.bit_length() - 1)
    )
    y = (turn - quadrant * quarter).astype(F32) * (2.0 * math.pi / samples)
    z = y * y
    s = y + y * z * (-1.6666654611e-1 + z * (8.3321608736e-3 - z * 1.9515295891e-4))
    c = 1.0 - 0.5 * z + z * z * (4.166664568298827e-2 + z * (-1.388731625493765e-3 + z * 2.443315711809948e-5))
    odd = (quadrant & 1) == 1
    cos_abs = jnp.where(odd, s, c)
    sin_abs = jnp.where(odd, c, s)
    cos = jnp.where(((quadrant + 1) & 2) == 2, -cos_abs, cos_abs)
    sin = jnp.where((quadrant & 2) == 2, -sin_abs, sin_abs)
    return cos, sin


def repeat(count, body):
    if count <= 8:
        for i in range(count):
            body(i)
    else:
        lax.fori_loop(0, count, lambda i, carry: (body(i), carry)[1], 0)


def multiple(value, of):
    return value if isinstance(value, int) else pl.multiple_of(value, of)


def lane_gather(values, at):
    dims = lax.GatherDimensionNumbers(
        offset_dims=(),
        collapsed_slice_dims=(1,),
        start_index_map=(1,),
        operand_batching_dims=(0,),
        start_indices_batching_dims=(0,),
    )
    return lax.gather(values, at[..., None], dims, (1, 1), mode=lax.GatherScatterMode.PROMISE_IN_BOUNDS)


def iota(shape, dim):
    return lax.broadcasted_iota(jnp.int32, shape, dim)


def shift(values, by):
    return lax.shift_right_logical(values, jnp.full_like(values, by))


STEP, FIRST = (2, 4, 8, 8), (1, 2, 4, 0)
RESIDUES = (0, 4, 2, 6, 1, 5, 3, 7)


def class_order():
    row, column = iota((LANES, LANES), 0), iota((LANES, LANES), 1)
    bin_of, first = jnp.full_like(row, 0), 0
    for step, start in zip(STEP, FIRST):
        bin_of = jnp.where(row >= first, step * (row - first) + start, bin_of)
        first += LANES // step
    return jnp.where(bin_of == column, 1.0, 0.0).astype(BF16)


def dedisperse_kernel(trials_each, dm_ref, cd_ref, sp_hbm, send_ref, keep_ref, sp, ph, turned, y0, y1, xs, sem):
    channels, bins = sp.shape[1:]
    samples = 2 * bins
    half = LANES // 2
    tiles = bins // LANES
    spread = bins // (8 * half)
    chunks = 8 * spread
    chan = lax.axis_index("chan")
    block = chan * lax.axis_size("bin") + lax.axis_index("bin")
    fetch = pltpu.make_async_copy(sp_hbm, sp, sem)
    fetch.start()

    if channels >= LANES:
        rows = [cd_ref[pl.ds(block * (channels // LANES) + k, 1), :] for k in range(channels // LANES)]
        cd = jnp.concatenate([jnp.broadcast_to(row, (LANES, LANES)).T for row in rows], axis=0)
    else:
        first = block * channels
        row = cd_ref[pl.ds(first // LANES, 1), :]
        moved = pltpu.roll(jnp.broadcast_to(row, (LANES, LANES)), (LANES - first % LANES) % LANES, 1)
        cd = moved.T[:channels]
    lane = iota(cd.shape, 1)
    start = 8 * (lane & (half - 1)) * cd - jnp.where(lane >= half, samples // 4, 0)
    du, dv = sincos(cd & (samples - 1), samples)
    for h in range(spread):
        u, v = sincos((start + 8 * half * h * cd) & (samples - 1), samples)
        for residue in range(8):
            value = u
            if h == 0 and residue == 0:
                value = jnp.where(lane == half, (1 - 2 * (cd & 1)).astype(F32), u)
            at = (RESIDUES.index(residue) * spread + h) * LANES
            ph[:, at : at + LANES] = value.astype(BF16)
            if residue < 7:
                u, v = u * du - v * dv, v * du + u * dv

    lane = iota((16, LANES), 1)
    trial = ((lane // (2 * trials_each)) ^ chan) * trials_each + (lane & (trials_each - 1))
    dm = jnp.concatenate([dm_ref[...], dm_ref[...]], axis=1)
    dm = jnp.take_along_axis(jnp.broadcast_to(dm, (16, LANES)), trial, axis=1)
    imag = (lane & trials_each) != 0
    row = iota((16, LANES), 0)
    own_half = jnp.where(imag, half, 0)
    edge = jnp.zeros((send_ref.shape[0], EDGE), BF16)
    for ref in (send_ref, keep_ref):
        ref[:, :EDGE] = edge
        ref[:, bins + EDGE :] = edge

    order = class_order()
    fetch.wait()
    starts = [sum(bins // s for s in STEP[:k]) for k in range(4)]

    def turn_tile(t):
        columns = pl.ds(multiple(t * LANES, LANES), LANES)
        for part in range(2):
            rows = lax.dot_general(order, sp[part, :, columns], (((1,), (1,)), ((), ())), preferred_element_type=F32)
            rows = rows.astype(BF16)
            first = 0
            for k in range(4):
                size = LANES // STEP[k]
                turned[part, pl.ds(multiple(starts[k] + t * size, 16), size), :] = rows[first : first + size]
                first += size

    repeat(tiles, turn_tile)

    def multiply(k, b, size, y):
        count = chunks >> k
        columns = count * LANES
        rows = pl.ds(multiple(starts[k] + b * size, 16), size)
        for part in range(2):
            y[part, :size, :columns] = jnp.dot(
                turned[part, rows, :], ph[:, :columns], preferred_element_type=F32
            ).astype(BF16)

    def pick(k, b, size, y):
        each = LANES // STEP[k]
        tile_first = sum(LANES // s for s in STEP[:k])

        def group(i):
            base = b * size + i * 16
            signed = ((STEP[k] * (base + row) + FIRST[k]) * dm + bins & (samples - 1)) - bins
            near = jnp.abs(signed)
            key = (near & (bins - 1 - 8 * (half - 1))).astype(jnp.int16)
            at_re = (shift(near, 3) & (half - 1)) ^ own_half ^ jnp.where(signed == -bins, half, 0)
            at_im = (at_re ^ half).astype(jnp.int16)
            at_re = at_re.astype(jnp.int16)
            got = []
            for part, at in ((0, at_re), (1, at_im)):
                value = None
                for j in range(chunks >> k):
                    lanes = slice(j * LANES, (j + 1) * LANES)
                    new = lane_gather(y[part, pl.ds(multiple(i * 16, 16), 16), lanes], at)
                    this = RESIDUES[j // spread] + 8 * half * (j % spread)
                    value = new if value is None else jnp.where(key == this, new, value)
                got.append(value.astype(F32))
            sign = jnp.where((signed & (bins - 1)) == 0, 0.0, jnp.where(signed < 0, -1.0, 1.0))
            total = got[0] * jnp.where(imag, -sign, 1.0) + got[1] * jnp.where(imag, 1.0, sign)
            at = (base // each) * LANES + tile_first + base % each
            xs[pl.ds(multiple(at, 16), 16), :] = total.astype(BF16)

        repeat(size // 16, group)

    size = y0.shape[1]
    work = [(k, b, min(size, bins // STEP[k])) for k in range(4) for b in range(max(1, bins // STEP[k] // size))]
    if len(work) <= 16:
        buffers = (y0, y1)
        multiply(*work[0], y0)
        for n, item in enumerate(work):
            if n + 1 < len(work):
                multiply(*work[n + 1], buffers[(n + 1) % 2])
            pick(*item, buffers[n % 2])
    else:
        for k in range(4):

            def whole_block(b, carry, k=k):
                multiply(k, b, min(size, bins // STEP[k]), y0)
                pick(k, b, min(size, bins // STEP[k]), y0)
                return carry

            lax.fori_loop(0, max(1, bins // STEP[k] // size), whole_block, 0)

    wide = 2 * trials_each

    def finish(t):
        rows = xs[pl.ds(multiple(t * LANES, LANES), LANES), :]
        out = lax.dot_general(rows, order, (((0,), (0,)), ((), ())), preferred_element_type=F32).astype(BF16)
        columns = pl.ds(multiple(EDGE + t * LANES, LANES), LANES)
        for k in range(LANES // wide):
            ref = (keep_ref, send_ref)[k % 2]
            ref[(k // 2) * wide : (k // 2 + 1) * wide, columns] = out[k * wide : (k + 1) * wide]

    repeat(tiles, finish)


def dedisperse(spectra, dm_trials, chan_delay, trials_each):
    _, channels, bins = spectra.shape
    size = 128
    rows = LANES // 2
    delays = chan_delay.reshape(-1, LANES)
    shape = jax.ShapeDtypeStruct((rows, bins + 2 * EDGE), BF16)
    in_vmem = pl.BlockSpec(memory_space=pltpu.VMEM)
    return pl.pallas_call(
        functools.partial(dedisperse_kernel, trials_each),
        in_specs=[in_vmem, in_vmem, pl.BlockSpec(memory_space=pl.ANY)],
        out_specs=[in_vmem] * 2,
        out_shape=[shape] * 2,
        scratch_shapes=[
            pltpu.VMEM(spectra.shape, BF16),
            pltpu.VMEM((channels, 2 * bins), BF16),
            pltpu.VMEM((2, bins, channels), BF16),
            pltpu.VMEM((2, size, 2 * bins), BF16),
            pltpu.VMEM((2, size, 2 * bins), BF16),
            pltpu.VMEM((bins, LANES), BF16),
            pltpu.SemaphoreType.DMA,
        ],
        compiler_params=pltpu.CompilerParams(vmem_limit_bytes=62 * 2**20),
        name="dedisperse",
    )(dm_trials.reshape(1, -1), delays, spectra)


def pick_kernel(bank_ref, ids_ref, out_ref):
    bank, taps = bank_ref.shape[1:]
    count = ids_ref.shape[1]
    rows = lax.broadcasted_iota(jnp.int32, (bank, count), 0)
    one_hot = jnp.where(rows == ids_ref[...], 1.0, 0.0).astype(BF16)
    at = lax.broadcasted_iota(jnp.int32, (taps, taps), 0)
    to = lax.broadcasted_iota(jnp.int32, (taps, taps), 1)
    flip = jnp.where(at == (to ^ 15), 1.0, 0.0).astype(BF16)
    chosen = []
    for part in range(2):
        taken = lax.dot_general(one_hot, bank_ref[part], (((0,), (0,)), ((), ())), preferred_element_type=F32)
        chosen.append(jnp.dot(taken.astype(BF16), flip, preferred_element_type=F32))
    re, im = chosen
    out_ref[:count, :taps] = re.astype(BF16)
    out_ref[:count, taps:] = (-im).astype(BF16)
    out_ref[count:, :taps] = im.astype(BF16)
    out_ref[count:, taps:] = re.astype(BF16)


def pick_templates(template_bank, template_ids):
    _, bank, taps = template_bank.shape
    count = template_ids.shape[0]
    return pl.pallas_call(
        pick_kernel,
        out_shape=jax.ShapeDtypeStruct((2 * count, 2 * taps), BF16),
        cost_estimate=pl.CostEstimate(flops=4 * count * bank * taps, bytes_accessed=2**20, transcendentals=0),
        name="pick_templates",
    )(template_bank, template_ids.reshape(1, -1))


def search_kernel(scale, taps, near_ref, far_ref, templates_ref, out_ref, signal, hankel):
    step = pl.program_id(0)
    each, count, bins = out_ref.shape
    rows, width = near_ref.shape
    trials = rows // 2

    @pl.when(step == 0)
    def _():
        total = near_ref[...].astype(F32) + far_ref[...].astype(F32)
        signal[...] = (total * scale).astype(BF16).astype(F32)

    for k in range(each):
        trial = step * each + k
        for part in range(2):
            line = signal[pl.ds(part * trials + trial, 1), :]
            skew = pltpu.roll(jnp.broadcast_to(line, (16, width)), width - 15, 1, stride=1, stride_axis=0)
            for e in range(LANES // 16):
                moved = skew if e == 0 else pltpu.roll(skew, width - 16 * e, 1)
                moved = moved.astype(BF16)
                for h in range(taps // LANES):
                    at = part * taps + h * LANES + 16 * e
                    hankel[k, at : at + 16, :] = moved[:, h * LANES : h * LANES + bins]
        response = jnp.dot(templates_ref[...], hankel[k], preferred_element_type=F32)
        re, im = response[:count], response[count:]
        out_ref[k] = (re * re + im * im).astype(BF16)


def search(near, far, templates, scale, bins):
    rows, width = near.shape
    trials = rows // 2
    taps = templates.shape[1] // 2
    count = templates.shape[0] // 2
    each = min(trials, 4)
    whole = lambda shape: pl.BlockSpec(shape, lambda i: (0,) * len(shape))
    return pl.pallas_call(
        functools.partial(search_kernel, scale, taps),
        grid=(trials // each,),
        in_specs=[whole(near.shape), whole(far.shape), whole(templates.shape)],
        out_specs=pl.BlockSpec((each, count, bins), lambda i: (i, 0, 0)),
        out_shape=jax.ShapeDtypeStruct((trials, count, bins), BF16),
        scratch_shapes=[pltpu.VMEM((rows, width), F32), pltpu.VMEM((each, 2 * taps, bins), BF16)],
        compiler_params=pltpu.CompilerParams(vmem_limit_bytes=48 * 2**20),
        name="search",
    )(near, far, templates)


def swap(cells, axis, distance):
    return lax.ppermute(cells, axis, [(i, i ^ distance) for i in range(lax.axis_size(axis))])


def local(spectra, dm_trials, chan_delay, template_bank, template_ids):
    owners, spans = lax.axis_size("chan"), lax.axis_size("bin")
    bins = spectra.shape[2]
    own_bins = bins // spans
    trials_each = dm_trials.shape[0] // owners
    scale = 1.0 / math.sqrt(chan_delay.shape[0])
    wide = 2 * trials_each
    templates = pick_templates(template_bank, template_ids)
    send, keep = dedisperse(spectra, dm_trials, chan_delay, trials_each)
    distance = 1
    while True:
        got = swap(send, "chan", distance)
        distance *= 2
        if distance == owners:
            break
        total = (keep.astype(F32) + got.astype(F32)).astype(BF16).reshape(-1, 2, wide, keep.shape[1])
        keep, send = total[:, 0].reshape(-1, keep.shape[1]), total[:, 1].reshape(-1, keep.shape[1])
    place = lax.axis_index("bin")
    part = spans // 2
    while part:
        total = (keep.astype(F32) + got.astype(F32)).astype(BF16)
        left, right = total[:, : part * own_bins + 2 * EDGE], total[:, part * own_bins :]
        upper = (place & part) != 0
        keep, send = jnp.where(upper, right, left), jnp.where(upper, left, right)
        got = swap(send, "bin", part)
        part //= 2
    return search(keep, got, templates, scale, own_bins)


def solution(mesh):
    in_specs = (P(None, ("beam", "chan", "bin"), None), P(), P(), P(), P())
    out_specs = P(("beam", "chan"), None, "bin")
    return jax.shard_map(local, mesh=mesh, in_specs=in_specs, out_specs=out_specs, check_vma=False)
```

```python
import functools
import math

import jax
import jax.numpy as jnp
from jax import lax
from jax.experimental import pallas as pl
from jax.experimental.pallas import tpu as pltpu
from jax.sharding import PartitionSpec as P

EDGE = 128
LANES = 128
SUB = 8
F32 = jnp.float32
BF16 = jnp.bfloat16


def sincos(turn, samples):
    quarter = samples // 4
    quadrant = (turn + quarter // 2) // quarter if quarter & (quarter - 1) else lax.shift_right_logical(
        turn + quarter // 2, jnp.full_like(turn, quarter.bit_length() - 1)
    )
    y = (turn - quadrant * quarter).astype(F32) * (2.0 * math.pi / samples)
    z = y * y
    s = y + y * z * (-1.6666654611e-1 + z * (8.3321608736e-3 - z * 1.9515295891e-4))
    c = 1.0 - 0.5 * z + z * z * (4.166664568298827e-2 + z * (-1.388731625493765e-3 + z * 2.443315711809948e-5))
    odd = (quadrant & 1) == 1
    cos_abs = jnp.where(odd, s, c)
    sin_abs = jnp.where(odd, c, s)
    cos = jnp.where(((quadrant + 1) & 2) == 2, -cos_abs, cos_abs)
    sin = jnp.where((quadrant & 2) == 2, -sin_abs, sin_abs)
    return cos, sin


def repeat(count, body):
    if count <= 8:
        for i in range(count):
            body(i)
    else:
        lax.fori_loop(0, count, lambda i, carry: (body(i), carry)[1], 0)


def multiple(value, of):
    return value if isinstance(value, int) else pl.multiple_of(value, of)


def lane_gather(values, at):
    dims = lax.GatherDimensionNumbers(
        offset_dims=(),
        collapsed_slice_dims=(1,),
        start_index_map=(1,),
        operand_batching_dims=(0,),
        start_indices_batching_dims=(0,),
    )
    return lax.gather(values, at[..., None], dims, (1, 1), mode=lax.GatherScatterMode.PROMISE_IN_BOUNDS)


def iota(shape, dim):
    return lax.broadcasted_iota(jnp.int32, shape, dim)


def shift(values, by):
    return lax.shift_right_logical(values, jnp.full_like(values, by))


STEP, FIRST = (2, 4, 8, 8), (1, 2, 4, 0)
RESIDUES = (0, 4, 2, 6, 1, 5, 3, 7)


def class_order():
    row, column = iota((LANES, LANES), 0), iota((LANES, LANES), 1)
    bin_of, first = jnp.full_like(row, 0), 0
    for step, start in zip(STEP, FIRST):
        bin_of = jnp.where(row >= first, step * (row - first) + start, bin_of)
        first += LANES // step
    return jnp.where(bin_of == column, 1.0, 0.0).astype(BF16)


def times(one, other):
    return one[0] * other[0] - one[1] * other[1], one[1] * other[0] + one[0] * other[1]


def dedisperse_kernel(
    trials_each, dm_hbm, cd_hbm, sp_hbm, send_ref, keep_ref, dm_ref, cd_ref, sp, ph, turned, y0, y1, xs, sems
):
    channels, bins = sp.shape[1:]
    samples = 2 * bins
    half = LANES // 2
    tiles = bins // LANES
    spread = bins // (8 * half)
    chunks = 8 * spread
    chan = lax.axis_index("chan")
    block = chan * lax.axis_size("bin") + lax.axis_index("bin")
    fetches = [
        pltpu.make_async_copy(source, target, sems.at[n])
        for n, (source, target) in enumerate(((cd_hbm, cd_ref), (sp_hbm, sp), (dm_hbm, dm_ref)))
    ]
    for fetch in fetches:
        fetch.start()
    order = class_order()
    edge = jnp.zeros((send_ref.shape[0], EDGE), BF16)
    for ref in (send_ref, keep_ref):
        ref[:, :EDGE] = edge
        ref[:, bins + EDGE :] = edge

    fetches[0].wait()
    if channels >= LANES:
        rows = [cd_ref[pl.ds(block * (channels // LANES) + k, 1), :] for k in range(channels // LANES)]
        cd = jnp.concatenate([jnp.broadcast_to(row, (LANES, LANES)).T for row in rows], axis=0)
    else:
        first = block * channels
        row = cd_ref[pl.ds(first // LANES, 1), :]
        moved = pltpu.roll(jnp.broadcast_to(row, (LANES, LANES)), (LANES - first % LANES) % LANES, 1)
        cd = moved.T[:channels]
    column = iota(cd.shape, 1)
    start = 8 * (column & (half - 1)) * cd - jnp.where(column >= half, samples // 4, 0)
    turns = {1: sincos(cd & (samples - 1), samples)}
    turns[2] = times(turns[1], turns[1])
    turns[4] = times(turns[2], turns[2])
    bases = [{0: sincos((start + 8 * half * h * cd) & (samples - 1), samples)} for h in range(spread)]

    def make_phases(residue):
        for h in range(spread):
            if residue:
                by = residue & -residue
                bases[h][residue] = times(bases[h][residue - by], turns[by])
            value = bases[h][residue][0]
            if h == 0 and residue == 0:
                value = jnp.where(column == half, (1 - 2 * (cd & 1)).astype(F32), value)
            at = (RESIDUES.index(residue) * spread + h) * LANES
            ph[:, at : at + LANES] = value.astype(BF16)

    make_phases(0)
    make_phases(4)
    fetches[2].wait()
    lane = iota((16, LANES), 1)
    trial = ((lane // (2 * trials_each)) ^ chan) * trials_each + (lane & (trials_each - 1))
    dm = jnp.concatenate([dm_ref[...], dm_ref[...]], axis=1)
    dm = jnp.take_along_axis(jnp.broadcast_to(dm, (16, LANES)), trial, axis=1)
    imag = (lane & trials_each) != 0
    row = iota((16, LANES), 0)
    own_half = jnp.where(imag, half, 0)
    starts = [sum(bins // s for s in STEP[:k]) for k in range(4)]
    fetches[1].wait()

    def turn_tile(t):
        columns = pl.ds(multiple(t * LANES, LANES), LANES)
        for part in range(2):
            rows = lax.dot_general(order, sp[part, :, columns], (((1,), (1,)), ((), ())), preferred_element_type=F32)
            rows = rows.astype(BF16)
            first = 0
            for k in range(4):
                size = LANES // STEP[k]
                turned[part, pl.ds(multiple(starts[k] + t * size, 16), size), :] = rows[first : first + size]
                first += size

    def multiply(k, b, size, y):
        columns = (chunks >> k) * LANES
        rows = pl.ds(multiple(starts[k] + b * size, 16), size)
        for part in range(2):
            y[part, :size, :columns] = jnp.dot(
                turned[part, rows, :], ph[:, :columns], preferred_element_type=F32
            ).astype(BF16)

    def pick(k, b, size, y):
        each = LANES // STEP[k]
        tile_first = sum(LANES // s for s in STEP[:k])

        def group(i):
            base = b * size + i * 16
            signed = ((STEP[k] * (base + row) + FIRST[k]) * dm + bins & (samples - 1)) - bins
            near = jnp.abs(signed)
            key = (near & (bins - 1 - 8 * (half - 1))).astype(jnp.int16)
            at_re = (shift(near, 3) & (half - 1)) ^ own_half ^ jnp.where(signed == -bins, half, 0)
            at_im = (at_re ^ half).astype(jnp.int16)
            at_re = at_re.astype(jnp.int16)
            got = []
            for part, at in ((0, at_re), (1, at_im)):
                value = None
                for j in range(chunks >> k):
                    lanes = slice(j * LANES, (j + 1) * LANES)
                    new = lane_gather(y[part, pl.ds(multiple(i * 16, 16), 16), lanes], at)
                    this = RESIDUES[j // spread] + 8 * half * (j % spread)
                    value = new if value is None else jnp.where(key == this, new, value)
                got.append(value.astype(F32))
            sign = jnp.where((signed & (bins - 1)) == 0, 0.0, jnp.where(signed < 0, -1.0, 1.0))
            total = got[0] * jnp.where(imag, -sign, 1.0) + got[1] * jnp.where(imag, 1.0, sign)
            at = (base // each) * LANES + tile_first + base % each
            xs[pl.ds(multiple(at, 16), 16), :] = total.astype(BF16)

        repeat(size // 16, group)

    wide = 2 * trials_each

    def finish(t):
        rows = xs[pl.ds(multiple(t * LANES, LANES), LANES), :]
        out = lax.dot_general(rows, order, (((0,), (0,)), ((), ())), preferred_element_type=F32).astype(BF16)
        columns = pl.ds(multiple(EDGE + t * LANES, LANES), LANES)
        for k in range(LANES // wide):
            ref = (keep_ref, send_ref)[k % 2]
            ref[(k // 2) * wide : (k // 2 + 1) * wide, columns] = out[k * wide : (k + 1) * wide]

    size = y0.shape[1]
    sizes = [min(size, bins // s) for s in STEP]
    counts = [bins // s // own for s, own in zip(STEP, sizes)]
    if tiles <= 8:
        work = [(k, b, sizes[k]) for k in (3, 2, 1, 0) for b in range(counts[k])]
        buffers = (y0, y1)
        for t in range(tiles):
            turn_tile(t)
        multiply(*work[0], y0)
        made = {}
        for residue in (2, 6, 1, 5, 3, 7):
            make_phases(residue)
        per_block = sizes[0] * STEP[0] // LANES
        for n, item in enumerate(work):
            for residue in made.get(n, ()):
                make_phases(residue)
            if n + 1 < len(work):
                multiply(*work[n + 1], buffers[(n + 1) % 2])
            pick(*item, buffers[n % 2])
            if item[0] == 0:
                for t in range(item[1] * per_block, (item[1] + 1) * per_block):
                    finish(t)
    else:
        for residue in (2, 6, 1, 5, 3, 7):
            make_phases(residue)
        repeat(tiles, turn_tile)
        for k in range(4):

            def whole_block(b, carry, k=k):
                multiply(k, b, sizes[k], y0)
                pick(k, b, sizes[k], y0)
                return carry

            lax.fori_loop(0, counts[k], whole_block, 0)
        repeat(tiles, finish)


def dedisperse(spectra, dm_trials, chan_delay, trials_each):
    _, channels, bins = spectra.shape
    size = 128
    rows = LANES // 2
    dm = dm_trials.reshape(1, -1)
    delays = chan_delay.reshape(-1, LANES)
    out = pltpu.VMEM((rows, bins + 2 * EDGE), BF16)
    room = 12 * rows * (bins + 2 * EDGE) * 2
    return pl.pallas_call(
        functools.partial(dedisperse_kernel, trials_each),
        in_specs=[pl.BlockSpec(memory_space=pltpu.HBM)] * 3,
        out_specs=[pl.BlockSpec(memory_space=pltpu.VMEM)] * 2,
        out_shape=[out] * 2,
        scratch_shapes=[
            pltpu.VMEM(dm.shape, jnp.int32),
            pltpu.VMEM(delays.shape, jnp.int32),
            pltpu.VMEM(spectra.shape, BF16),
            pltpu.VMEM((channels, 2 * bins), BF16),
            pltpu.VMEM((2, bins, channels), BF16),
            pltpu.VMEM((2, size, 2 * bins), BF16),
            pltpu.VMEM((2, size, 2 * bins), BF16),
            pltpu.VMEM((bins, LANES), BF16),
            pltpu.SemaphoreType.DMA((3,)),
        ],
        compiler_params=pltpu.CompilerParams(vmem_limit_bytes=min(62 * 2**20, 64 * 2**20 - room)),
        name="dedisperse",
    )(dm, delays, spectra)


def pick_kernel(bank_ref, ids_ref, out_ref):
    bank, taps = bank_ref.shape[1:]
    count = ids_ref.shape[1]
    rows = lax.broadcasted_iota(jnp.int32, (bank, count), 0)
    one_hot = jnp.where(rows == ids_ref[...], 1.0, 0.0).astype(BF16)
    at = lax.broadcasted_iota(jnp.int32, (taps, taps), 0)
    to = lax.broadcasted_iota(jnp.int32, (taps, taps), 1)
    flip = jnp.where(at == (to ^ 15), 1.0, 0.0).astype(BF16)
    chosen = []
    for part in range(2):
        taken = lax.dot_general(one_hot, bank_ref[part], (((0,), (0,)), ((), ())), preferred_element_type=F32)
        chosen.append(jnp.dot(taken.astype(BF16), flip, preferred_element_type=F32))
    re, im = chosen
    out_ref[:count, :taps] = re.astype(BF16)
    out_ref[:count, taps:] = (-im).astype(BF16)
    out_ref[count:, :taps] = im.astype(BF16)
    out_ref[count:, taps:] = re.astype(BF16)


def pick_templates(template_bank, template_ids):
    _, bank, taps = template_bank.shape
    count = template_ids.shape[0]
    return pl.pallas_call(
        pick_kernel,
        out_shape=pltpu.VMEM((2 * count, 2 * taps), BF16),
        cost_estimate=pl.CostEstimate(flops=4 * count * bank * taps, bytes_accessed=2**20, transcendentals=0),
        name="pick_templates",
    )(template_bank, template_ids.reshape(1, -1))


def search_kernel(scale, near_ref, far_ref, templates_ref, out_hbm, signal, hankel, out, sems):
    trials, count, bins = out.shape
    width = near_ref.shape[1]
    taps = templates_ref.shape[1] // 2
    total = near_ref[...].astype(F32) + far_ref[...].astype(F32)
    signal[...] = (total * scale).astype(BF16).astype(F32)
    each = trials // sems.shape[0]
    ahead = iota((16, LANES), 1) + 15 - iota((16, LANES), 0)
    ats = [(ahead + 16 * e & (LANES - 1)).astype(jnp.int16) for e in range(LANES // 16)]
    stays = [(ahead + 16 * e).astype(jnp.int16) < LANES for e in range(LANES // 16)]

    def fill(trial, to):
        for part in range(2):
            line = signal[pl.ds(part * trials + trial, 1), :]
            line = jnp.broadcast_to(line, (16, width)).astype(BF16)
            pieces = [line[:, v * LANES : (v + 1) * LANES] for v in range(width // LANES)]
            for e in range(LANES // 16):
                turned = [lane_gather(piece, ats[e]) for piece in pieces]
                moved = [jnp.where(stays[e], turned[v], turned[v + 1]) for v in range(len(turned) - 1)]
                for h in range(taps // LANES):
                    at = part * taps + h * LANES + 16 * e
                    for v in range(bins // LANES):
                        to[at : at + 16, v * LANES : (v + 1) * LANES] = moved[h + v]

    copies = []
    for trial in range(trials):
        fill(trial, hankel.at[trial % 2])
        response = jnp.dot(templates_ref[...], hankel[trial % 2], preferred_element_type=F32)
        re, im = response[:count], response[count:]
        out[trial] = (re * re + im * im).astype(BF16)
        if trial % each == each - 1:
            here = pl.ds(trial + 1 - each, each)
            copies.append(pltpu.make_async_copy(out.at[here], out_hbm.at[here], sems.at[trial // each]))
            copies[-1].start()
    for copy in copies:
        copy.wait()


def search(near, far, templates, scale, bins):
    rows, width = near.shape
    trials = rows // 2
    taps = templates.shape[1] // 2
    count = templates.shape[0] // 2
    in_vmem = pl.BlockSpec(memory_space=pltpu.VMEM)
    return pl.pallas_call(
        functools.partial(search_kernel, scale),
        in_specs=[in_vmem] * 3,
        out_specs=pl.BlockSpec(memory_space=pltpu.HBM),
        out_shape=jax.ShapeDtypeStruct((trials, count, bins), BF16),
        scratch_shapes=[
            pltpu.VMEM((rows, width), F32),
            pltpu.VMEM((2, 2 * taps, bins), BF16),
            pltpu.VMEM((trials, count, bins), BF16),
            pltpu.SemaphoreType.DMA((min(trials, 4),)),
        ],
        compiler_params=pltpu.CompilerParams(vmem_limit_bytes=32 * 2**20),
        name="search",
    )(near, far, templates)


def swap(cells, axis, distance):
    return lax.ppermute(cells, axis, [(i, i ^ distance) for i in range(lax.axis_size(axis))])


def local(spectra, dm_trials, chan_delay, template_bank, template_ids):
    owners, spans = lax.axis_size("chan"), lax.axis_size("bin")
    bins = spectra.shape[2]
    own_bins = bins // spans
    trials_each = dm_trials.shape[0] // owners
    scale = 1.0 / math.sqrt(chan_delay.shape[0])
    wide = 2 * trials_each
    templates = pick_templates(template_bank, template_ids)
    send, keep = dedisperse(spectra, dm_trials, chan_delay, trials_each)
    distance = 1
    while True:
        got = swap(send, "chan", distance)
        distance *= 2
        if distance == owners:
            break
        total = (keep.astype(F32) + got.astype(F32)).astype(BF16).reshape(-1, 2, wide, keep.shape[1])
        keep, send = total[:, 0].reshape(-1, keep.shape[1]), total[:, 1].reshape(-1, keep.shape[1])
    place = lax.axis_index("bin")
    part = spans // 2
    while part:
        total = (keep.astype(F32) + got.astype(F32)).astype(BF16)
        left, right = total[:, : part * own_bins + 2 * EDGE], total[:, part * own_bins :]
        upper = (place & part) != 0
        keep, send = jnp.where(upper, right, left), jnp.where(upper, left, right)
        got = swap(send, "bin", part)
        part //= 2
    return search(keep, got, templates, scale, own_bins)


def solution(mesh):
    in_specs = (P(None, ("beam", "chan", "bin"), None), P(), P(), P(), P())
    out_specs = P(("beam", "chan"), None, "bin")
    return jax.shard_map(local, mesh=mesh, in_specs=in_specs, out_specs=out_specs, check_vma=False)
```

```python
import functools
import math

import jax
import jax.numpy as jnp
from jax import lax
from jax.experimental import pallas as pl
from jax.experimental.pallas import tpu as pltpu
from jax.sharding import PartitionSpec as P

EDGE = 128
LANES = 128
SUB = 8
F32 = jnp.float32
BF16 = jnp.bfloat16


def sincos(turn, samples):
    quarter = samples // 4
    quadrant = (turn + quarter // 2) // quarter if quarter & (quarter - 1) else lax.shift_right_logical(
        turn + quarter // 2, jnp.full_like(turn, quarter.bit_length() - 1)
    )
    y = (turn - quadrant * quarter).astype(F32) * (2.0 * math.pi / samples)
    z = y * y
    s = y + y * z * (-1.6666654611e-1 + z * (8.3321608736e-3 - z * 1.9515295891e-4))
    c = 1.0 - 0.5 * z + z * z * (4.166664568298827e-2 + z * (-1.388731625493765e-3 + z * 2.443315711809948e-5))
    odd = (quadrant & 1) == 1
    cos_abs = jnp.where(odd, s, c)
    sin_abs = jnp.where(odd, c, s)
    cos = jnp.where(((quadrant + 1) & 2) == 2, -cos_abs, cos_abs)
    sin = jnp.where((quadrant & 2) == 2, -sin_abs, sin_abs)
    return cos, sin


def repeat(count, body):
    if count <= 8:
        for i in range(count):
            body(i)
    else:
        lax.fori_loop(0, count, lambda i, carry: (body(i), carry)[1], 0)


def multiple(value, of):
    return value if isinstance(value, int) else pl.multiple_of(value, of)


def lane_gather(values, at):
    dims = lax.GatherDimensionNumbers(
        offset_dims=(),
        collapsed_slice_dims=(1,),
        start_index_map=(1,),
        operand_batching_dims=(0,),
        start_indices_batching_dims=(0,),
    )
    return lax.gather(values, at[..., None], dims, (1, 1), mode=lax.GatherScatterMode.PROMISE_IN_BOUNDS)


def iota(shape, dim):
    return lax.broadcasted_iota(jnp.int32, shape, dim)


def shift(values, by):
    return lax.shift_right_logical(values, jnp.full_like(values, by))


STEP, FIRST = (2, 4, 8, 8), (1, 2, 4, 0)
RESIDUES = (0, 4, 2, 6, 1, 5, 3, 7)


def class_order():
    row, column = iota((LANES, LANES), 0), iota((LANES, LANES), 1)
    bin_of, first = jnp.full_like(row, 0), 0
    for step, start in zip(STEP, FIRST):
        bin_of = jnp.where(row >= first, step * (row - first) + start, bin_of)
        first += LANES // step
    return jnp.where(bin_of == column, 1.0, 0.0).astype(BF16)


def quarter_turns(value, count):
    odd = (count & 1) == 1
    cos, sin = jnp.where(odd, value[1], value[0]), jnp.where(odd, value[0], value[1])
    return jnp.where(((count + 1) & 2) == 2, -cos, cos), jnp.where((count & 2) == 2, -sin, sin)


def times(one, other):
    return one[0] * other[0] - one[1] * other[1], one[1] * other[0] + one[0] * other[1]


def dedisperse_kernel(
    trials_each, dm_hbm, cd_hbm, sp_hbm, send_ref, keep_ref, dm_ref, cd_ref, sp, ph, turned, y0, y1, xs, sems
):
    channels, bins = sp.shape[1:]
    samples = 2 * bins
    half = LANES // 2
    tiles = bins // LANES
    spread = bins // (8 * half)
    chunks = 8 * spread
    chan = lax.axis_index("chan")
    block = chan * lax.axis_size("bin") + lax.axis_index("bin")
    fetches = [
        pltpu.make_async_copy(source, target, sems.at[n])
        for n, (source, target) in enumerate(((cd_hbm, cd_ref), (sp_hbm, sp), (dm_hbm, dm_ref)))
    ]
    for fetch in fetches:
        fetch.start()
    order = class_order()
    edge = jnp.zeros((send_ref.shape[0], EDGE), BF16)
    for ref in (send_ref, keep_ref):
        ref[:, :EDGE] = edge
        ref[:, bins + EDGE :] = edge

    fetches[0].wait()
    if channels >= LANES:
        rows = [cd_ref[pl.ds(block * (channels // LANES) + k, 1), :] for k in range(channels // LANES)]
        cd = jnp.concatenate([jnp.broadcast_to(row, (LANES, LANES)).T for row in rows], axis=0)
    else:
        first = block * channels
        row = cd_ref[pl.ds(first // LANES, 1), :]
        moved = pltpu.roll(jnp.broadcast_to(row, (LANES, LANES)), (LANES - first % LANES) % LANES, 1)
        cd = moved.T[:channels]
    column = iota(cd.shape, 1)
    start = 8 * (column & (half - 1)) * cd - jnp.where(column >= half, samples // 4, 0)
    turns = {1: sincos(cd & (samples - 1), samples)}
    turns[2] = times(turns[1], turns[1])
    turns[4] = times(turns[2], turns[2])
    bases = [{0: sincos(start & (samples - 1), samples)}]
    for h in range(1, spread):
        if 8 * half * h * 4 == samples:
            bases.append({0: quarter_turns(bases[0][0], cd)})
        else:
            bases.append({0: sincos((start + 8 * half * h * cd) & (samples - 1), samples)})

    def make_phases(residue):
        for h in range(spread):
            if residue:
                by = residue & -residue
                bases[h][residue] = times(bases[h][residue - by], turns[by])
            value = bases[h][residue][0]
            if h == 0 and residue == 0:
                value = jnp.where(column == half, (1 - 2 * (cd & 1)).astype(F32), value)
            at = (RESIDUES.index(residue) * spread + h) * LANES
            ph[:, at : at + LANES] = value.astype(BF16)

    make_phases(0)
    make_phases(4)
    fetches[2].wait()
    lane = iota((16, LANES), 1)
    trial = ((lane // (2 * trials_each)) ^ chan) * trials_each + (lane & (trials_each - 1))
    dm = jnp.concatenate([dm_ref[...], dm_ref[...]], axis=1)
    dm = jnp.take_along_axis(jnp.broadcast_to(dm, (16, LANES)), trial, axis=1)
    imag = (lane & trials_each).astype(jnp.int16) != 0
    row = iota((16, LANES), 0)
    own_half = jnp.where((lane & trials_each) != 0, half, 0).astype(jnp.int16)
    other_half = own_half ^ half
    zero, one = jnp.zeros((16, LANES), BF16), jnp.ones((16, LANES), BF16)
    running = {}
    starts = [sum(bins // s for s in STEP[:k]) for k in range(4)]
    fetches[1].wait()

    def turn_tile(t):
        columns = pl.ds(multiple(t * LANES, LANES), LANES)
        for part in range(2):
            rows = lax.dot_general(order, sp[part, :, columns], (((1,), (1,)), ((), ())), preferred_element_type=F32)
            rows = rows.astype(BF16)
            first = 0
            for k in range(4):
                size = LANES // STEP[k]
                turned[part, pl.ds(multiple(starts[k] + t * size, 16), size), :] = rows[first : first + size]
                first += size

    def multiply(k, b, size, y):
        columns = (chunks >> k) * LANES
        rows = pl.ds(multiple(starts[k] + b * size, 16), size)
        for part in range(2):
            for at in range(0, columns, 256):
                y[part, :size, at : at + 256] = jnp.dot(
                    turned[part, rows, :], ph[:, at : at + 256], preferred_element_type=F32
                ).astype(BF16)

    def pick(k, b, size, y):
        each = LANES // STEP[k]
        tile_first = sum(LANES // s for s in STEP[:k])

        begin = ((STEP[k] * row + FIRST[k]) * dm).astype(jnp.int16)
        more = (16 * STEP[k] * dm).astype(jnp.int16)

        def group(i, product=None):
            base = b * size + i * 16
            if product is None:
                product = ((STEP[k] * (base + row) + FIRST[k]) * dm).astype(jnp.int16)
            unused = 16 - samples.bit_length() + 1
            signed = lax.shift_left(product, jnp.full_like(product, unused))
            signed = lax.shift_right_arithmetic(signed, jnp.full_like(signed, unused))
            near = jnp.abs(signed)
            key = near & (bins - 1 - 8 * (half - 1))
            at_re = (shift(near, 3) & (half - 1)) ^ jnp.where(signed == -bins, other_half, own_half)
            at_im = at_re ^ half
            got = []
            for part, at in ((0, at_re), (1, at_im)):
                value = None
                for j in range(chunks >> k):
                    lanes = slice(j * LANES, (j + 1) * LANES)
                    new = lane_gather(y[part, pl.ds(multiple(i * 16, 16), 16), lanes], at)
                    this = RESIDUES[j // spread] + 8 * half * (j % spread)
                    value = new if value is None else jnp.where(key == this, new, value)
                got.append(value)
            sign = jnp.where(signed < 0, -one, one)
            sign = jnp.where((signed & (bins - 1)) == 0, zero, sign)
            total = got[0] * jnp.where(imag, -sign, one) + got[1] * jnp.where(imag, one, sign)
            at = (base // each) * LANES + tile_first + base % each
            xs[pl.ds(multiple(at, 16), 16), :] = total
            return product

        if isinstance(b, int) and size // 16 <= 8:
            product = running.get(k, begin)
            for i in range(size // 16):
                group(i, product)
                product = product + more
            running[k] = product
            return
        repeat(size // 16, group)

    wide = 2 * trials_each

    def finish(t):
        rows = xs[pl.ds(multiple(t * LANES, LANES), LANES), :]
        out = lax.dot_general(rows, order, (((0,), (0,)), ((), ())), preferred_element_type=F32).astype(BF16)
        columns = pl.ds(multiple(EDGE + t * LANES, LANES), LANES)
        for k in range(LANES // wide):
            ref = (keep_ref, send_ref)[k % 2]
            ref[(k // 2) * wide : (k // 2 + 1) * wide, columns] = out[k * wide : (k + 1) * wide]

    size = y0.shape[1]
    sizes = [min(size, bins // s) for s in STEP]
    counts = [bins // s // own for s, own in zip(STEP, sizes)]
    if tiles <= 8:
        work = [(k, b, sizes[k]) for k in (3, 2, 1, 0) for b in range(counts[k])]
        buffers = (y0, y1)
        for t in range(tiles):
            turn_tile(t)
        multiply(*work[0], y0)
        made = {}
        for residue in (2, 6, 1, 5, 3, 7):
            make_phases(residue)
        per_block = sizes[0] * STEP[0] // LANES
        for n, item in enumerate(work):
            for residue in made.get(n, ()):
                make_phases(residue)
            if n + 1 < len(work):
                multiply(*work[n + 1], buffers[(n + 1) % 2])
            pick(*item, buffers[n % 2])
            if item[0] == 0:
                for t in range(item[1] * per_block, (item[1] + 1) * per_block):
                    finish(t)
    else:
        for residue in (2, 6, 1, 5, 3, 7):
            make_phases(residue)
        repeat(tiles, turn_tile)
        for k in range(4):

            def whole_block(b, carry, k=k):
                multiply(k, b, sizes[k], y0)
                pick(k, b, sizes[k], y0)
                return carry

            lax.fori_loop(0, counts[k], whole_block, 0)
        repeat(tiles, finish)


def dedisperse(spectra, dm_trials, chan_delay, trials_each):
    _, channels, bins = spectra.shape
    size = 128
    rows = LANES // 2
    dm = dm_trials.reshape(1, -1)
    delays = chan_delay.reshape(-1, LANES)
    out = pltpu.VMEM((rows, bins + 2 * EDGE), BF16)
    room = 12 * rows * (bins + 2 * EDGE) * 2
    return pl.pallas_call(
        functools.partial(dedisperse_kernel, trials_each),
        in_specs=[pl.BlockSpec(memory_space=pltpu.HBM)] * 3,
        out_specs=[pl.BlockSpec(memory_space=pltpu.VMEM)] * 2,
        out_shape=[out] * 2,
        scratch_shapes=[
            pltpu.VMEM(dm.shape, jnp.int32),
            pltpu.VMEM(delays.shape, jnp.int32),
            pltpu.VMEM(spectra.shape, BF16),
            pltpu.VMEM((channels, 2 * bins), BF16),
            pltpu.VMEM((2, bins, channels), BF16),
            pltpu.VMEM((2, size, 2 * bins), BF16),
            pltpu.VMEM((2, size, 2 * bins), BF16),
            pltpu.VMEM((bins, LANES), BF16),
            pltpu.SemaphoreType.DMA((3,)),
        ],
        compiler_params=pltpu.CompilerParams(vmem_limit_bytes=min(62 * 2**20, 64 * 2**20 - room)),
        name="dedisperse",
    )(dm, delays, spectra)


def pick_kernel(bank_ref, ids_ref, out_ref):
    bank, taps = bank_ref.shape[1:]
    count = ids_ref.shape[1]
    rows = lax.broadcasted_iota(jnp.int32, (bank, count), 0)
    one_hot = jnp.where(rows == ids_ref[...], 1.0, 0.0).astype(BF16)
    at = lax.broadcasted_iota(jnp.int32, (taps, taps), 0)
    to = lax.broadcasted_iota(jnp.int32, (taps, taps), 1)
    flip = jnp.where(at == (to ^ 15), 1.0, 0.0).astype(BF16)
    chosen = []
    for part in range(2):
        taken = lax.dot_general(one_hot, bank_ref[part], (((0,), (0,)), ((), ())), preferred_element_type=F32)
        chosen.append(jnp.dot(taken.astype(BF16), flip, preferred_element_type=F32))
    re, im = chosen
    out_ref[:count, :taps] = re.astype(BF16)
    out_ref[:count, taps:] = (-im).astype(BF16)
    out_ref[count:, :taps] = im.astype(BF16)
    out_ref[count:, taps:] = re.astype(BF16)


def pick_templates(template_bank, template_ids):
    _, bank, taps = template_bank.shape
    count = template_ids.shape[0]
    return pl.pallas_call(
        pick_kernel,
        out_shape=pltpu.VMEM((2 * count, 2 * taps), BF16),
        cost_estimate=pl.CostEstimate(flops=4 * count * bank * taps, bytes_accessed=2**20, transcendentals=0),
        name="pick_templates",
    )(template_bank, template_ids.reshape(1, -1))


def search_kernel(scale, near_ref, far_ref, templates_ref, out_hbm, signal, hankel, out, sems):
    trials, count, bins = out.shape
    width = near_ref.shape[1]
    taps = templates_ref.shape[1] // 2
    total = near_ref[...].astype(F32) + far_ref[...].astype(F32)
    signal[...] = (total * scale).astype(BF16).astype(F32)
    each = trials // sems.shape[0]
    ahead = iota((16, LANES), 1) + 15 - iota((16, LANES), 0)
    ats = [(ahead + 16 * e & (LANES - 1)).astype(jnp.int16) for e in range(LANES // 16)]
    stays = [(ahead + 16 * e).astype(jnp.int16) < LANES for e in range(LANES // 16)]

    def fill(trial, to):
        for part in range(2):
            line = signal[pl.ds(part * trials + trial, 1), :]
            line = jnp.broadcast_to(line, (16, width)).astype(BF16)
            pieces = [line[:, v * LANES : (v + 1) * LANES] for v in range(width // LANES)]
            for e in range(LANES // 16):
                turned = [lane_gather(piece, ats[e]) for piece in pieces]
                moved = [jnp.where(stays[e], turned[v], turned[v + 1]) for v in range(len(turned) - 1)]
                for h in range(taps // LANES):
                    at = part * taps + h * LANES + 16 * e
                    for v in range(bins // LANES):
                        to[at : at + 16, v * LANES : (v + 1) * LANES] = moved[h + v]

    copies = []
    for trial in range(trials):
        fill(trial, hankel.at[trial % 2])
        response = jnp.dot(templates_ref[...], hankel[trial % 2], preferred_element_type=F32)
        re, im = response[:count], response[count:]
        out[trial] = (re * re + im * im).astype(BF16)
        if trial % each == each - 1:
            here = pl.ds(trial + 1 - each, each)
            copies.append(pltpu.make_async_copy(out.at[here], out_hbm.at[here], sems.at[trial // each]))
            copies[-1].start()
    for copy in copies:
        copy.wait()


def search(near, far, templates, scale, bins):
    rows, width = near.shape
    trials = rows // 2
    taps = templates.shape[1] // 2
    count = templates.shape[0] // 2
    in_vmem = pl.BlockSpec(memory_space=pltpu.VMEM)
    return pl.pallas_call(
        functools.partial(search_kernel, scale),
        in_specs=[in_vmem] * 3,
        out_specs=pl.BlockSpec(memory_space=pltpu.HBM),
        out_shape=jax.ShapeDtypeStruct((trials, count, bins), BF16),
        scratch_shapes=[
            pltpu.VMEM((rows, width), F32),
            pltpu.VMEM((2, 2 * taps, bins), BF16),
            pltpu.VMEM((trials, count, bins), BF16),
            pltpu.SemaphoreType.DMA((min(trials, 4),)),
        ],
        compiler_params=pltpu.CompilerParams(vmem_limit_bytes=32 * 2**20),
        name="search",
    )(near, far, templates)


def swap(cells, owner_bit, span_bit):
    owners, spans = lax.axis_size("chan"), lax.axis_size("bin")
    pairs = [(i, i ^ (span_bit * owners + owner_bit)) for i in range(owners * spans)]
    return lax.ppermute(cells, ("bin", "chan"), pairs)


def add(*cells):
    return sum(cell.astype(F32) for cell in cells).astype(BF16)


def local(spectra, dm_trials, chan_delay, template_bank, template_ids):
    owners, spans = lax.axis_size("chan"), lax.axis_size("bin")
    bins = spectra.shape[2]
    own_bins = bins // spans
    trials_each = dm_trials.shape[0] // owners
    scale = 1.0 / math.sqrt(chan_delay.shape[0])
    wide = 2 * trials_each
    place = lax.axis_index("bin")
    templates = pick_templates(template_bank, template_ids)
    send, keep = dedisperse(spectra, dm_trials, chan_delay, trials_each)
    distance = 1
    while 2 * distance < owners:
        total = add(keep, swap(send, distance, 0)).reshape(-1, 2, wide, keep.shape[1])
        keep, send = total[:, 0].reshape(-1, keep.shape[1]), total[:, 1].reshape(-1, keep.shape[1])
        distance *= 2
    reach = (spans - 1) * own_bins + 2 * EDGE
    odd = (place & 1) != 0

    def by_parity(cells):
        low, high = cells[:, :reach], cells[:, own_bins : own_bins + reach]
        return jnp.where(odd, high, low), jnp.where(odd, low, high)

    keep, keep_far = by_parity(keep)
    send, send_far = by_parity(send)
    keep = add(keep, swap(send, distance, 0), swap(keep_far, 0, 1), swap(send_far, distance, 1))
    part = spans // 2
    while True:
        width = (part // 2 - 1) * 2 * own_bins + own_bins + 2 * EDGE
        upper = (place & part) != 0
        left, right = keep[:, :width], keep[:, part * own_bins : part * own_bins + width]
        keep, send = jnp.where(upper, right, left), jnp.where(upper, left, right)
        got = swap(send, 0, part)
        if part == 2:
            return search(keep, got, templates, scale, own_bins)
        keep = add(keep, got)
        part //= 2


def solution(mesh):
    in_specs = (P(None, ("beam", "chan", "bin"), None), P(), P(), P(), P())
    out_specs = P(("beam", "chan"), None, "bin")
    return jax.shard_map(local, mesh=mesh, in_specs=in_specs, out_specs=out_specs, check_vma=False)
```

```python
import functools
import math

import jax
import jax.numpy as jnp
from jax import lax
from jax.experimental import pallas as pl
from jax.experimental.pallas import tpu as pltpu
from jax.sharding import PartitionSpec as P

EDGE = 128
LANES = 128
SUB = 8
F32 = jnp.float32
BF16 = jnp.bfloat16


def sincos(turn, samples):
    quarter = samples // 4
    quadrant = (turn + quarter // 2) // quarter if quarter & (quarter - 1) else lax.shift_right_logical(
        turn + quarter // 2, jnp.full_like(turn, quarter.bit_length() - 1)
    )
    y = (turn - quadrant * quarter).astype(F32) * (2.0 * math.pi / samples)
    z = y * y
    s = y + y * z * (-1.6666654611e-1 + z * (8.3321608736e-3 - z * 1.9515295891e-4))
    c = 1.0 - 0.5 * z + z * z * (4.166664568298827e-2 + z * (-1.388731625493765e-3 + z * 2.443315711809948e-5))
    odd = (quadrant & 1) == 1
    cos_abs = jnp.where(odd, s, c)
    sin_abs = jnp.where(odd, c, s)
    cos = jnp.where(((quadrant + 1) & 2) == 2, -cos_abs, cos_abs)
    sin = jnp.where((quadrant & 2) == 2, -sin_abs, sin_abs)
    return cos, sin


def repeat(count, body):
    if count <= 8:
        for i in range(count):
            body(i)
    else:
        lax.fori_loop(0, count, lambda i, carry: (body(i), carry)[1], 0)


def multiple(value, of):
    return value if isinstance(value, int) else pl.multiple_of(value, of)


def lane_gather(values, at):
    dims = lax.GatherDimensionNumbers(
        offset_dims=(),
        collapsed_slice_dims=(1,),
        start_index_map=(1,),
        operand_batching_dims=(0,),
        start_indices_batching_dims=(0,),
    )
    return lax.gather(values, at[..., None], dims, (1, 1), mode=lax.GatherScatterMode.PROMISE_IN_BOUNDS)


def iota(shape, dim):
    return lax.broadcasted_iota(jnp.int32, shape, dim)


def shift(values, by):
    return lax.shift_right_logical(values, jnp.full_like(values, by))


STEP, FIRST = (2, 4, 8, 8), (1, 2, 4, 0)
RESIDUES = (0, 4, 2, 6, 1, 5, 3, 7)


def class_order():
    row, column = iota((LANES, LANES), 0), iota((LANES, LANES), 1)
    bin_of, first = jnp.full_like(row, 0), 0
    for step, start in zip(STEP, FIRST):
        bin_of = jnp.where(row >= first, step * (row - first) + start, bin_of)
        first += LANES // step
    return jnp.where(bin_of == column, 1.0, 0.0).astype(BF16)


def quarter_turns(value, count):
    odd = (count & 1) == 1
    cos, sin = jnp.where(odd, value[1], value[0]), jnp.where(odd, value[0], value[1])
    return jnp.where(((count + 1) & 2) == 2, -cos, cos), jnp.where((count & 2) == 2, -sin, sin)


def times(one, other):
    return one[0] * other[0] - one[1] * other[1], one[1] * other[0] + one[0] * other[1]


def dedisperse_kernel(
    trials_each, dm_hbm, cd_hbm, sp_hbm, send_ref, keep_ref, dm_ref, cd_ref, sp, ph, turned, y0, y1, xs, sems
):
    channels, bins = sp.shape[1:]
    samples = 2 * bins
    half = LANES // 2
    tiles = bins // LANES
    spread = bins // (8 * half)
    chunks = 8 * spread
    chan = lax.axis_index("chan")
    block = chan * lax.axis_size("bin") + lax.axis_index("bin")
    fetches = [
        pltpu.make_async_copy(source, target, sems.at[n])
        for n, (source, target) in enumerate(((cd_hbm, cd_ref), (sp_hbm, sp), (dm_hbm, dm_ref)))
    ]
    for fetch in fetches:
        fetch.start()
    order = class_order()
    edge = jnp.zeros((send_ref.shape[0], EDGE), BF16)
    for ref in (send_ref, keep_ref):
        ref[:, :EDGE] = edge
        ref[:, bins + EDGE :] = edge

    fetches[0].wait()
    if channels >= LANES:
        rows = [cd_ref[pl.ds(block * (channels // LANES) + k, 1), :] for k in range(channels // LANES)]
        cd = jnp.concatenate([jnp.broadcast_to(row, (LANES, LANES)).T for row in rows], axis=0)
    else:
        first = block * channels
        row = cd_ref[pl.ds(first // LANES, 1), :]
        moved = pltpu.roll(jnp.broadcast_to(row, (LANES, LANES)), (LANES - first % LANES) % LANES, 1)
        cd = moved.T[:channels]
    column = iota(cd.shape, 1)
    start = 8 * (column & (half - 1)) * cd - jnp.where(column >= half, samples // 4, 0)
    turns = {1: sincos(cd & (samples - 1), samples)}
    turns[2] = times(turns[1], turns[1])
    turns[4] = times(turns[2], turns[2])
    bases = [{0: sincos(start & (samples - 1), samples)}]
    for h in range(1, spread):
        if 8 * half * h * 4 == samples:
            bases.append({0: quarter_turns(bases[0][0], cd)})
        else:
            bases.append({0: sincos((start + 8 * half * h * cd) & (samples - 1), samples)})

    def make_phases(residue):
        for h in range(spread):
            if residue:
                by = residue & -residue
                bases[h][residue] = times(bases[h][residue - by], turns[by])
            value = bases[h][residue][0]
            if h == 0 and residue == 0:
                value = jnp.where(column == half, (1 - 2 * (cd & 1)).astype(F32), value)
            at = (RESIDUES.index(residue) * spread + h) * LANES
            ph[:, at : at + LANES] = value.astype(BF16)

    make_phases(0)
    make_phases(4)
    fetches[2].wait()
    lane = iota((16, LANES), 1)
    trial = ((lane // (2 * trials_each)) ^ chan) * trials_each + (lane & (trials_each - 1))
    dm = jnp.concatenate([dm_ref[...], dm_ref[...]], axis=1)
    dm = jnp.take_along_axis(jnp.broadcast_to(dm, (16, LANES)), trial, axis=1)
    imag = (lane & trials_each).astype(jnp.int16) != 0
    row = iota((16, LANES), 0)
    own_half = jnp.where((lane & trials_each) != 0, half, 0).astype(jnp.int16)
    other_half = own_half ^ half
    zero, one = jnp.zeros((16, LANES), BF16), jnp.ones((16, LANES), BF16)
    running = {}
    starts = [sum(bins // s for s in STEP[:k]) for k in range(4)]
    fetches[1].wait()

    def turn_tile(t):
        columns = pl.ds(multiple(t * LANES, LANES), LANES)
        for part in range(2):
            rows = lax.dot_general(order, sp[part, :, columns], (((1,), (1,)), ((), ())), preferred_element_type=F32)
            rows = rows.astype(BF16)
            first = 0
            for k in range(4):
                size = LANES // STEP[k]
                turned[part, pl.ds(multiple(starts[k] + t * size, 16), size), :] = rows[first : first + size]
                first += size

    def multiply(k, b, size, y):
        columns = (chunks >> k) * LANES
        rows = pl.ds(multiple(starts[k] + b * size, 16), size)
        for part in range(2):
            for at in range(0, columns, 256):
                y[part, :size, at : at + 256] = jnp.dot(
                    turned[part, rows, :], ph[:, at : at + 256], preferred_element_type=F32
                ).astype(BF16)

    def pick(k, b, size, y):
        each = LANES // STEP[k]
        tile_first = sum(LANES // s for s in STEP[:k])

        begin = ((STEP[k] * row + FIRST[k]) * dm).astype(jnp.int16)
        more = (16 * STEP[k] * dm).astype(jnp.int16)

        def group(i, product=None):
            base = b * size + i * 16
            if product is None:
                product = ((STEP[k] * (base + row) + FIRST[k]) * dm).astype(jnp.int16)
            unused = 16 - samples.bit_length() + 1
            signed = lax.shift_left(product, jnp.full_like(product, unused))
            signed = lax.shift_right_arithmetic(signed, jnp.full_like(signed, unused))
            near = jnp.abs(signed)
            key = near & (bins - 1 - 8 * (half - 1))
            at_re = (shift(near, 3) & (half - 1)) ^ jnp.where(signed == -bins, other_half, own_half)
            at_im = at_re ^ half
            got = []
            for part, at in ((0, at_re), (1, at_im)):
                value = None
                for j in range(chunks >> k):
                    lanes = slice(j * LANES, (j + 1) * LANES)
                    new = lane_gather(y[part, pl.ds(multiple(i * 16, 16), 16), lanes], at)
                    this = RESIDUES[j // spread] + 8 * half * (j % spread)
                    value = new if value is None else jnp.where(key == this, new, value)
                got.append(value)
            sign = jnp.where(signed < 0, -one, one)
            sign = jnp.where((signed & (bins - 1)) == 0, zero, sign)
            total = got[0] * jnp.where(imag, -sign, one) + got[1] * jnp.where(imag, one, sign)
            at = (base // each) * LANES + tile_first + base % each
            xs[pl.ds(multiple(at, 16), 16), :] = total
            return product

        if isinstance(b, int) and size // 16 <= 8:
            product = running.get(k, begin)
            for i in range(size // 16):
                group(i, product)
                product = product + more
            running[k] = product
            return
        repeat(size // 16, group)

    wide = 2 * trials_each

    def finish(t):
        rows = xs[pl.ds(multiple(t * LANES, LANES), LANES), :]
        out = lax.dot_general(rows, order, (((0,), (0,)), ((), ())), preferred_element_type=F32).astype(BF16)
        columns = pl.ds(multiple(EDGE + t * LANES, LANES), LANES)
        for k in range(LANES // wide):
            ref = (keep_ref, send_ref)[k % 2]
            ref[(k // 2) * wide : (k // 2 + 1) * wide, columns] = out[k * wide : (k + 1) * wide]

    size = y0.shape[1]
    sizes = [min(size, bins // s) for s in STEP]
    counts = [bins // s // own for s, own in zip(STEP, sizes)]
    if tiles <= 8:
        work = [(k, b, sizes[k]) for k in (3, 2, 1, 0) for b in range(counts[k])]
        buffers = (y0, y1)
        for t in range(tiles):
            turn_tile(t)
        multiply(*work[0], y0)
        made = {}
        for residue in (2, 6, 1, 5, 3, 7):
            make_phases(residue)
        per_block = sizes[0] * STEP[0] // LANES
        for n, item in enumerate(work):
            for residue in made.get(n, ()):
                make_phases(residue)
            if n + 1 < len(work):
                multiply(*work[n + 1], buffers[(n + 1) % 2])
            pick(*item, buffers[n % 2])
            if item[0] == 0:
                for t in range(item[1] * per_block, (item[1] + 1) * per_block):
                    finish(t)
    else:
        for residue in (2, 6, 1, 5, 3, 7):
            make_phases(residue)
        repeat(tiles, turn_tile)
        for k in range(4):

            def whole_block(b, carry, k=k):
                multiply(k, b, sizes[k], y0)
                pick(k, b, sizes[k], y0)
                return carry

            lax.fori_loop(0, counts[k], whole_block, 0)
        repeat(tiles, finish)


def dedisperse(spectra, dm_trials, chan_delay, trials_each):
    _, channels, bins = spectra.shape
    size = 128
    rows = LANES // 2
    dm = dm_trials.reshape(1, -1)
    delays = chan_delay.reshape(-1, LANES)
    out = pltpu.VMEM((rows, bins + 2 * EDGE), BF16)
    room = 12 * rows * (bins + 2 * EDGE) * 2
    return pl.pallas_call(
        functools.partial(dedisperse_kernel, trials_each),
        in_specs=[pl.BlockSpec(memory_space=pltpu.HBM)] * 3,
        out_specs=[pl.BlockSpec(memory_space=pltpu.VMEM)] * 2,
        out_shape=[out] * 2,
        scratch_shapes=[
            pltpu.VMEM(dm.shape, jnp.int32),
            pltpu.VMEM(delays.shape, jnp.int32),
            pltpu.VMEM(spectra.shape, BF16),
            pltpu.VMEM((channels, 2 * bins), BF16),
            pltpu.VMEM((2, bins, channels), BF16),
            pltpu.VMEM((2, size, 2 * bins), BF16),
            pltpu.VMEM((2, size, 2 * bins), BF16),
            pltpu.VMEM((bins, LANES), BF16),
            pltpu.SemaphoreType.DMA((3,)),
        ],
        compiler_params=pltpu.CompilerParams(vmem_limit_bytes=min(62 * 2**20, 64 * 2**20 - room)),
        name="dedisperse",
    )(dm, delays, spectra)


def pick_kernel(bank_ref, ids_ref, out_ref):
    bank, taps = bank_ref.shape[1:]
    count = ids_ref.shape[1]
    rows = lax.broadcasted_iota(jnp.int32, (bank, count), 0)
    one_hot = jnp.where(rows == ids_ref[...], 1.0, 0.0).astype(BF16)
    at = lax.broadcasted_iota(jnp.int32, (taps, taps), 0)
    to = lax.broadcasted_iota(jnp.int32, (taps, taps), 1)
    flip = jnp.where(at == (to ^ 15), 1.0, 0.0).astype(BF16)
    chosen = []
    for part in range(2):
        taken = lax.dot_general(one_hot, bank_ref[part], (((0,), (0,)), ((), ())), preferred_element_type=F32)
        chosen.append(jnp.dot(taken.astype(BF16), flip, preferred_element_type=F32))
    re, im = chosen
    out_ref[:count, :taps] = re.astype(BF16)
    out_ref[:count, taps:] = (-im).astype(BF16)
    out_ref[count:, :taps] = im.astype(BF16)
    out_ref[count:, taps:] = re.astype(BF16)


def pick_templates(template_bank, template_ids):
    _, bank, taps = template_bank.shape
    count = template_ids.shape[0]
    return pl.pallas_call(
        pick_kernel,
        out_shape=pltpu.VMEM((2 * count, 2 * taps), BF16),
        cost_estimate=pl.CostEstimate(flops=4 * count * bank * taps, bytes_accessed=2**20, transcendentals=0),
        name="pick_templates",
    )(template_bank, template_ids.reshape(1, -1))


def search_kernel(scale, near_ref, far_ref, templates_ref, out_hbm, signal, out, sems):
    trials, count, bins = out.shape
    width = near_ref.shape[1]
    taps = templates_ref.shape[1] // 2
    total = near_ref[...].astype(F32) + far_ref[...].astype(F32)
    signal[...] = (total * scale).astype(BF16).astype(F32)
    each = trials // sems.shape[0]
    ahead = iota((16, LANES), 1) + 15 - iota((16, LANES), 0)
    ats = [(ahead + 16 * e & (LANES - 1)).astype(jnp.int16) for e in range(LANES // 16)]
    stays = [(ahead + 16 * e).astype(jnp.int16) < LANES for e in range(LANES // 16)]

    def fill(trial, part):
        line = signal[pl.ds(part * trials + trial, 1), :]
        line = jnp.broadcast_to(line, (16, width)).astype(BF16)
        pieces = [line[:, v * LANES : (v + 1) * LANES] for v in range(width // LANES)]
        moved = []
        for e in range(LANES // 16):
            turned = [lane_gather(piece, ats[e]) for piece in pieces]
            moved.append([jnp.where(stays[e], turned[v], turned[v + 1]) for v in range(len(turned) - 1)])
        rows = []
        for h in range(taps // LANES):
            for e in range(LANES // 16):
                rows.append(jnp.concatenate([moved[e][h + v] for v in range(bins // LANES)], axis=1))
        return jnp.concatenate(rows, axis=0)

    copies = []
    for trial in range(trials):
        response = sum(
            jnp.dot(templates_ref[:, part * taps : (part + 1) * taps], fill(trial, part), preferred_element_type=F32)
            for part in range(2)
        )
        re, im = response[:count], response[count:]
        out[trial] = (re * re + im * im).astype(BF16)
        if trial % each == each - 1:
            here = pl.ds(trial + 1 - each, each)
            copies.append(pltpu.make_async_copy(out.at[here], out_hbm.at[here], sems.at[trial // each]))
            copies[-1].start()
    for copy in copies:
        copy.wait()


def search(near, far, templates, scale, bins):
    rows, width = near.shape
    trials = rows // 2
    taps = templates.shape[1] // 2
    count = templates.shape[0] // 2
    in_vmem = pl.BlockSpec(memory_space=pltpu.VMEM)
    return pl.pallas_call(
        functools.partial(search_kernel, scale),
        in_specs=[in_vmem] * 3,
        out_specs=pl.BlockSpec(memory_space=pltpu.HBM),
        out_shape=jax.ShapeDtypeStruct((trials, count, bins), BF16),
        scratch_shapes=[
            pltpu.VMEM((rows, width), F32),
            pltpu.VMEM((trials, count, bins), BF16),
            pltpu.SemaphoreType.DMA((min(trials, 4),)),
        ],
        compiler_params=pltpu.CompilerParams(vmem_limit_bytes=32 * 2**20),
        name="search",
    )(near, far, templates)


def swap(cells, owner_bit, span_bit):
    owners, spans = lax.axis_size("chan"), lax.axis_size("bin")
    pairs = [(i, i ^ (span_bit * owners + owner_bit)) for i in range(owners * spans)]
    return lax.ppermute(cells, ("bin", "chan"), pairs)


def add(*cells):
    return sum(cell.astype(F32) for cell in cells).astype(BF16)


def local(spectra, dm_trials, chan_delay, template_bank, template_ids):
    owners, spans = lax.axis_size("chan"), lax.axis_size("bin")
    bins = spectra.shape[2]
    own_bins = bins // spans
    trials_each = dm_trials.shape[0] // owners
    scale = 1.0 / math.sqrt(chan_delay.shape[0])
    wide = 2 * trials_each
    place = lax.axis_index("bin")
    templates = pick_templates(template_bank, template_ids)
    send, keep = dedisperse(spectra, dm_trials, chan_delay, trials_each)
    distance = 1
    while 2 * distance < owners:
        total = add(keep, swap(send, distance, 0)).reshape(-1, 2, wide, keep.shape[1])
        keep, send = total[:, 0].reshape(-1, keep.shape[1]), total[:, 1].reshape(-1, keep.shape[1])
        distance *= 2
    reach = (spans - 1) * own_bins + 2 * EDGE
    odd = (place & 1) != 0

    def by_parity(cells):
        low, high = cells[:, :reach], cells[:, own_bins : own_bins + reach]
        return jnp.where(odd, high, low), jnp.where(odd, low, high)

    keep, keep_far = by_parity(keep)
    send, send_far = by_parity(send)
    send_far, keep_far, send = lax.optimization_barrier((send_far, keep_far, send))
    keep = add(keep, swap(send_far, distance, 1), swap(keep_far, 0, 1), swap(send, distance, 0))
    part = spans // 2
    while True:
        width = (part // 2 - 1) * 2 * own_bins + own_bins + 2 * EDGE
        upper = (place & part) != 0
        left, right = keep[:, :width], keep[:, part * own_bins : part * own_bins + width]
        keep, send = jnp.where(upper, right, left), jnp.where(upper, left, right)
        got = swap(send, 0, part)
        if part == 2:
            return search(keep, got, templates, scale, own_bins)
        keep = add(keep, got)
        part //= 2


def solution(mesh):
    in_specs = (P(None, ("beam", "chan", "bin"), None), P(), P(), P(), P())
    out_specs = P(("beam", "chan"), None, "bin")
    return jax.shard_map(local, mesh=mesh, in_specs=in_specs, out_specs=out_specs, check_vma=False)
```

```python
import functools
import math

import jax
import jax.numpy as jnp
from jax import lax
from jax.experimental import pallas as pl
from jax.experimental.pallas import tpu as pltpu
from jax.sharding import PartitionSpec as P

EDGE = 128
LANES = 128
SUB = 8
F32 = jnp.float32
BF16 = jnp.bfloat16


def sincos(turn, samples):
    quarter = samples // 4
    quadrant = (turn + quarter // 2) // quarter if quarter & (quarter - 1) else lax.shift_right_logical(
        turn + quarter // 2, jnp.full_like(turn, quarter.bit_length() - 1)
    )
    y = (turn - quadrant * quarter).astype(F32) * (2.0 * math.pi / samples)
    z = y * y
    s = y + y * z * (-1.6666654611e-1 + z * (8.3321608736e-3 - z * 1.9515295891e-4))
    c = 1.0 - 0.5 * z + z * z * (4.166664568298827e-2 + z * (-1.388731625493765e-3 + z * 2.443315711809948e-5))
    odd = (quadrant & 1) == 1
    cos_abs = jnp.where(odd, s, c)
    sin_abs = jnp.where(odd, c, s)
    cos = jnp.where(((quadrant + 1) & 2) == 2, -cos_abs, cos_abs)
    sin = jnp.where((quadrant & 2) == 2, -sin_abs, sin_abs)
    return cos, sin


def repeat(count, body):
    if count <= 8:
        for i in range(count):
            body(i)
    else:
        lax.fori_loop(0, count, lambda i, carry: (body(i), carry)[1], 0)


def multiple(value, of):
    return value if isinstance(value, int) else pl.multiple_of(value, of)


def lane_gather(values, at):
    dims = lax.GatherDimensionNumbers(
        offset_dims=(),
        collapsed_slice_dims=(1,),
        start_index_map=(1,),
        operand_batching_dims=(0,),
        start_indices_batching_dims=(0,),
    )
    return lax.gather(values, at[..., None], dims, (1, 1), mode=lax.GatherScatterMode.PROMISE_IN_BOUNDS)


def iota(shape, dim):
    return lax.broadcasted_iota(jnp.int32, shape, dim)


def shift(values, by):
    return lax.shift_right_logical(values, jnp.full_like(values, by))


STEP, FIRST = (2, 4, 8, 8), (1, 2, 4, 0)
RESIDUES = (0, 4, 2, 6, 1, 5, 3, 7)


def class_order():
    row, column = iota((LANES, LANES), 0), iota((LANES, LANES), 1)
    bin_of, first = jnp.full_like(row, 0), 0
    for step, start in zip(STEP, FIRST):
        bin_of = jnp.where(row >= first, step * (row - first) + start, bin_of)
        first += LANES // step
    return jnp.where(bin_of == column, 1.0, 0.0).astype(BF16)


def quarter_turns(value, count):
    odd = (count & 1) == 1
    cos, sin = jnp.where(odd, value[1], value[0]), jnp.where(odd, value[0], value[1])
    return jnp.where(((count + 1) & 2) == 2, -cos, cos), jnp.where((count & 2) == 2, -sin, sin)


def times(one, other):
    return one[0] * other[0] - one[1] * other[1], one[1] * other[0] + one[0] * other[1]


def dedisperse_kernel(
    trials_each, dm_hbm, cd_hbm, sp_hbm, send_ref, keep_ref, dm_ref, cd_ref, sp, ph, turned, y0, y1, xs, sems
):
    channels, bins = sp.shape[1:]
    samples = 2 * bins
    half = LANES // 2
    tiles = bins // LANES
    spread = bins // (8 * half)
    chunks = 8 * spread
    chan = lax.axis_index("chan")
    block = chan * lax.axis_size("bin") + lax.axis_index("bin")
    fetches = [
        pltpu.make_async_copy(source, target, sems.at[n])
        for n, (source, target) in enumerate(((cd_hbm, cd_ref), (sp_hbm, sp), (dm_hbm, dm_ref)))
    ]
    for fetch in fetches:
        fetch.start()
    order = class_order()
    edge = jnp.zeros((send_ref.shape[0], EDGE), BF16)
    for ref in (send_ref, keep_ref):
        ref[:, :EDGE] = edge
        ref[:, bins + EDGE :] = edge

    fetches[0].wait()
    if channels >= LANES:
        lines = [cd_ref[pl.ds(block * (channels // LANES) + k, 1), :] for k in range(channels // LANES)]
    else:
        first = block * channels
        line = cd_ref[pl.ds(first // LANES, 1), :]
        lines = [pltpu.roll(jnp.broadcast_to(line, (SUB, LANES)), (LANES - first % LANES) % LANES, 1)[:1]]

    def to_column(lines):
        return jnp.concatenate([jnp.broadcast_to(line, (LANES, LANES)).T for line in lines], axis=0)[:channels]

    cd = to_column(lines)
    own_turns = [sincos(line & (samples - 1), samples) for line in lines]
    column = iota(cd.shape, 1)
    start = 8 * (column & (half - 1)) * cd - jnp.where(column >= half, samples // 4, 0)
    turns = {1: tuple(to_column([turn[n] for turn in own_turns]) for n in range(2))}
    turns[2] = times(turns[1], turns[1])
    turns[4] = times(turns[2], turns[2])
    bases = [{0: sincos(start & (samples - 1), samples)}]
    for h in range(1, spread):
        if 8 * half * h * 4 == samples:
            bases.append({0: quarter_turns(bases[0][0], cd)})
        else:
            bases.append({0: sincos((start + 8 * half * h * cd) & (samples - 1), samples)})

    def make_phases(residue):
        for h in range(spread):
            if residue:
                by = residue & -residue
                bases[h][residue] = times(bases[h][residue - by], turns[by])
            value = bases[h][residue][0]
            if h == 0 and residue == 0:
                value = jnp.where(column == half, (1 - 2 * (cd & 1)).astype(F32), value)
            at = (RESIDUES.index(residue) * spread + h) * LANES
            ph[:, at : at + LANES] = value.astype(BF16)

    for residue in (0, 4, 2, 6, 1, 5, 3, 7):
        make_phases(residue)
    fetches[1].wait()
    fetches[2].wait()
    lane = iota((16, LANES), 1)
    trial = ((lane // (2 * trials_each)) ^ chan) * trials_each + (lane & (trials_each - 1))
    dm = jnp.concatenate([dm_ref[...], dm_ref[...]], axis=1)
    dm = jnp.take_along_axis(jnp.broadcast_to(dm, (16, LANES)), trial, axis=1)
    imag = (lane & trials_each).astype(jnp.int16) != 0
    row = iota((16, LANES), 0)
    own_half = jnp.where((lane & trials_each) != 0, half, 0).astype(jnp.int16)
    other_half = own_half ^ half
    zero, one = jnp.zeros((16, LANES), BF16), jnp.ones((16, LANES), BF16)
    running = {}
    starts = [sum(bins // s for s in STEP[:k]) for k in range(4)]

    def turn_tile(t):
        columns = pl.ds(multiple(t * LANES, LANES), LANES)
        for part in range(2):
            rows = lax.dot_general(order, sp[part, :, columns], (((1,), (1,)), ((), ())), preferred_element_type=F32)
            rows = rows.astype(BF16)
            first = 0
            for k in range(4):
                size = LANES // STEP[k]
                turned[part, pl.ds(multiple(starts[k] + t * size, 16), size), :] = rows[first : first + size]
                first += size

    def multiply(k, b, size, y):
        columns = (chunks >> k) * LANES
        rows = pl.ds(multiple(starts[k] + b * size, 16), size)
        for part in range(2):
            for at in range(0, columns, 256):
                y[part, :size, at : at + 256] = jnp.dot(
                    turned[part, rows, :], ph[:, at : at + 256], preferred_element_type=F32
                ).astype(BF16)

    def pick(k, b, size, y):
        each = LANES // STEP[k]
        tile_first = sum(LANES // s for s in STEP[:k])

        begin = ((STEP[k] * row + FIRST[k]) * dm).astype(jnp.int16)
        more = (16 * STEP[k] * dm).astype(jnp.int16)

        def group(i, product=None):
            base = b * size + i * 16
            if product is None:
                product = ((STEP[k] * (base + row) + FIRST[k]) * dm).astype(jnp.int16)
            unused = 16 - samples.bit_length() + 1
            signed = lax.shift_left(product, jnp.full_like(product, unused))
            signed = lax.shift_right_arithmetic(signed, jnp.full_like(signed, unused))
            near = jnp.abs(signed)
            key = near & (bins - 1 - 8 * (half - 1))
            at_re = (shift(near, 3) & (half - 1)) ^ jnp.where(signed == -bins, other_half, own_half)
            at_im = at_re ^ half
            got = []
            for part, at in ((0, at_re), (1, at_im)):
                value = None
                for j in range(chunks >> k):
                    lanes = slice(j * LANES, (j + 1) * LANES)
                    new = lane_gather(y[part, pl.ds(multiple(i * 16, 16), 16), lanes], at)
                    this = RESIDUES[j // spread] + 8 * half * (j % spread)
                    value = new if value is None else jnp.where(key == this, new, value)
                got.append(value)
            sign = jnp.where(signed < 0, -one, one)
            sign = jnp.where((signed & (bins - 1)) == 0, zero, sign)
            total = got[0] * jnp.where(imag, -sign, one) + got[1] * jnp.where(imag, one, sign)
            at = (base // each) * LANES + tile_first + base % each
            xs[pl.ds(multiple(at, 16), 16), :] = total
            return product

        if isinstance(b, int) and size // 16 <= 8:
            product = running.get(k, begin)
            for i in range(size // 16):
                group(i, product)
                product = product + more
            running[k] = product
            return
        repeat(size // 16, group)

    wide = 2 * trials_each

    def finish(t):
        rows = xs[pl.ds(multiple(t * LANES, LANES), LANES), :]
        out = lax.dot_general(rows, order, (((0,), (0,)), ((), ())), preferred_element_type=F32).astype(BF16)
        columns = pl.ds(multiple(EDGE + t * LANES, LANES), LANES)
        for k in range(LANES // wide):
            ref = (keep_ref, send_ref)[k % 2]
            ref[(k // 2) * wide : (k // 2 + 1) * wide, columns] = out[k * wide : (k + 1) * wide]

    size = y0.shape[1]
    sizes = [min(size, bins // s) for s in STEP]
    counts = [bins // s // own for s, own in zip(STEP, sizes)]
    if tiles <= 8:
        work = [(k, b, sizes[k]) for k in (0, 1, 2, 3) for b in range(counts[k])]
        buffers = (y0, y1)
        for t in range(tiles):
            turn_tile(t)
        multiply(*work[0], y0)
        for n, item in enumerate(work):
            if n + 1 < len(work):
                multiply(*work[n + 1], buffers[(n + 1) % 2])
            pick(*item, buffers[n % 2])
        for t in range(tiles):
            finish(t)
    else:
        repeat(tiles, turn_tile)
        for k in range(4):

            def whole_block(b, carry, k=k):
                multiply(k, b, sizes[k], y0)
                pick(k, b, sizes[k], y0)
                return carry

            lax.fori_loop(0, counts[k], whole_block, 0)
        repeat(tiles, finish)


def dedisperse(spectra, dm_trials, chan_delay, trials_each):
    _, channels, bins = spectra.shape
    size = 128
    rows = LANES // 2
    dm = dm_trials.reshape(1, -1)
    delays = chan_delay.reshape(-1, LANES)
    out = pltpu.VMEM((rows, bins + 2 * EDGE), BF16)
    room = 12 * rows * (bins + 2 * EDGE) * 2
    return pl.pallas_call(
        functools.partial(dedisperse_kernel, trials_each),
        in_specs=[pl.BlockSpec(memory_space=pltpu.HBM)] * 3,
        out_specs=[pl.BlockSpec(memory_space=pltpu.VMEM)] * 2,
        out_shape=[out] * 2,
        scratch_shapes=[
            pltpu.VMEM(dm.shape, jnp.int32),
            pltpu.VMEM(delays.shape, jnp.int32),
            pltpu.VMEM(spectra.shape, BF16),
            pltpu.VMEM((channels, 2 * bins), BF16),
            pltpu.VMEM((2, bins, channels), BF16),
            pltpu.VMEM((2, size, 2 * bins), BF16),
            pltpu.VMEM((2, size, 2 * bins), BF16),
            pltpu.VMEM((bins, LANES), BF16),
            pltpu.SemaphoreType.DMA((3,)),
        ],
        compiler_params=pltpu.CompilerParams(vmem_limit_bytes=min(62 * 2**20, 64 * 2**20 - room)),
        name="dedisperse",
    )(dm, delays, spectra)


def pick_kernel(bank_ref, ids_ref, out_ref):
    bank, taps = bank_ref.shape[1:]
    count = ids_ref.shape[1]
    rows = lax.broadcasted_iota(jnp.int32, (bank, count), 0)
    one_hot = jnp.where(rows == ids_ref[...], 1.0, 0.0).astype(BF16)
    at = lax.broadcasted_iota(jnp.int32, (taps, taps), 0)
    to = lax.broadcasted_iota(jnp.int32, (taps, taps), 1)
    flip = jnp.where(at == (to ^ 15), 1.0, 0.0).astype(BF16)
    chosen = []
    for part in range(2):
        taken = lax.dot_general(one_hot, bank_ref[part], (((0,), (0,)), ((), ())), preferred_element_type=F32)
        chosen.append(jnp.dot(taken.astype(BF16), flip, preferred_element_type=F32))
    re, im = chosen
    out_ref[:count, :taps] = re.astype(BF16)
    out_ref[:count, taps:] = (-im).astype(BF16)
    out_ref[count:, :taps] = im.astype(BF16)
    out_ref[count:, taps:] = re.astype(BF16)


def pick_templates(template_bank, template_ids):
    _, bank, taps = template_bank.shape
    count = template_ids.shape[0]
    return pl.pallas_call(
        pick_kernel,
        out_shape=pltpu.VMEM((2 * count, 2 * taps), BF16),
        cost_estimate=pl.CostEstimate(flops=4 * count * bank * taps, bytes_accessed=2**20, transcendentals=0),
        name="pick_templates",
    )(template_bank, template_ids.reshape(1, -1))


def search_kernel(scale, near_ref, far_ref, templates_ref, out_hbm, signal, out, sems):
    trials, count, bins = out.shape
    width = near_ref.shape[1]
    taps = templates_ref.shape[1] // 2
    total = near_ref[...].astype(F32) + far_ref[...].astype(F32)
    signal[...] = (total * scale).astype(BF16).astype(F32)
    each = trials // sems.shape[0]
    ahead = iota((16, LANES), 1) + 15 - iota((16, LANES), 0)
    ats = [(ahead + 16 * e & (LANES - 1)).astype(jnp.int16) for e in range(LANES // 16)]
    stays = [(ahead + 16 * e).astype(jnp.int16) < LANES for e in range(LANES // 16)]

    def fill(trial, part):
        line = signal[pl.ds(part * trials + trial, 1), :]
        line = jnp.broadcast_to(line, (16, width)).astype(BF16)
        pieces = [line[:, v * LANES : (v + 1) * LANES] for v in range(width // LANES)]
        moved = []
        for e in range(LANES // 16):
            turned = [lane_gather(piece, ats[e]) for piece in pieces]
            moved.append([jnp.where(stays[e], turned[v], turned[v + 1]) for v in range(len(turned) - 1)])
        rows = []
        for h in range(taps // LANES):
            for e in range(LANES // 16):
                rows.append(jnp.concatenate([moved[e][h + v] for v in range(bins // LANES)], axis=1))
        return jnp.concatenate(rows, axis=0)

    copies = []
    for trial in range(trials):
        response = sum(
            jnp.dot(templates_ref[:, part * taps : (part + 1) * taps], fill(trial, part), preferred_element_type=F32)
            for part in range(2)
        )
        re, im = response[:count], response[count:]
        out[trial] = (re * re + im * im).astype(BF16)
        if trial % each == each - 1:
            here = pl.ds(trial + 1 - each, each)
            copies.append(pltpu.make_async_copy(out.at[here], out_hbm.at[here], sems.at[trial // each]))
            copies[-1].start()
    for copy in copies:
        copy.wait()


def search(near, far, templates, scale, bins):
    rows, width = near.shape
    trials = rows // 2
    taps = templates.shape[1] // 2
    count = templates.shape[0] // 2
    in_vmem = pl.BlockSpec(memory_space=pltpu.VMEM)
    return pl.pallas_call(
        functools.partial(search_kernel, scale),
        in_specs=[in_vmem] * 3,
        out_specs=pl.BlockSpec(memory_space=pltpu.HBM),
        out_shape=jax.ShapeDtypeStruct((trials, count, bins), BF16),
        scratch_shapes=[
            pltpu.VMEM((rows, width), F32),
            pltpu.VMEM((trials, count, bins), BF16),
            pltpu.SemaphoreType.DMA((min(trials, 4),)),
        ],
        compiler_params=pltpu.CompilerParams(vmem_limit_bytes=32 * 2**20),
        name="search",
    )(near, far, templates)


def swap(cells, owner_bit, span_bit):
    owners, spans = lax.axis_size("chan"), lax.axis_size("bin")
    pairs = [(i, i ^ (span_bit * owners + owner_bit)) for i in range(owners * spans)]
    return lax.ppermute(cells, ("bin", "chan"), pairs)


def add(*cells):
    return sum(cell.astype(F32) for cell in cells).astype(BF16)


def local(spectra, dm_trials, chan_delay, template_bank, template_ids):
    owners, spans = lax.axis_size("chan"), lax.axis_size("bin")
    bins = spectra.shape[2]
    own_bins = bins // spans
    trials_each = dm_trials.shape[0] // owners
    scale = 1.0 / math.sqrt(chan_delay.shape[0])
    wide = 2 * trials_each
    place = lax.axis_index("bin")
    templates = pick_templates(template_bank, template_ids)
    send, keep = dedisperse(spectra, dm_trials, chan_delay, trials_each)
    distance = 1
    while 2 * distance < owners:
        total = add(keep, swap(send, distance, 0)).reshape(-1, 2, wide, keep.shape[1])
        keep, send = total[:, 0].reshape(-1, keep.shape[1]), total[:, 1].reshape(-1, keep.shape[1])
        distance *= 2
    reach = (spans - 1) * own_bins + 2 * EDGE
    odd = (place & 1) != 0

    def by_parity(cells):
        low, high = cells[:, :reach], cells[:, own_bins : own_bins + reach]
        return jnp.where(odd, high, low), jnp.where(odd, low, high)

    keep, keep_far = by_parity(keep)
    send, send_far = by_parity(send)
    send_far, keep_far, send = lax.optimization_barrier((send_far, keep_far, send))
    keep = add(keep, swap(send_far, distance, 1), swap(keep_far, 0, 1), swap(send, distance, 0))
    part = spans // 2
    while True:
        width = (part // 2 - 1) * 2 * own_bins + own_bins + 2 * EDGE
        upper = (place & part) != 0
        left, right = keep[:, :width], keep[:, part * own_bins : part * own_bins + width]
        keep, send = jnp.where(upper, right, left), jnp.where(upper, left, right)
        got = swap(send, 0, part)
        if part == 2:
            return search(keep, got, templates, scale, own_bins)
        keep = add(keep, got)
        part //= 2


def solution(mesh):
    in_specs = (P(None, ("beam", "chan", "bin"), None), P(), P(), P(), P())
    out_specs = P(("beam", "chan"), None, "bin")
    return jax.shard_map(local, mesh=mesh, in_specs=in_specs, out_specs=out_specs, check_vma=False)
```

```python
import functools
import math

import jax
import jax.numpy as jnp
from jax import lax
from jax.experimental import pallas as pl
from jax.experimental.pallas import tpu as pltpu
from jax.sharding import PartitionSpec as P

EDGE = 128
LANES = 128
SUB = 8
F32 = jnp.float32
BF16 = jnp.bfloat16


def sincos(turn, samples):
    quarter = samples // 4
    quadrant = (turn + quarter // 2) // quarter if quarter & (quarter - 1) else lax.shift_right_logical(
        turn + quarter // 2, jnp.full_like(turn, quarter.bit_length() - 1)
    )
    y = (turn - quadrant * quarter).astype(F32) * (2.0 * math.pi / samples)
    z = y * y
    s = y + y * z * (-1.6666654611e-1 + z * (8.3321608736e-3 - z * 1.9515295891e-4))
    c = 1.0 - 0.5 * z + z * z * (4.166664568298827e-2 + z * (-1.388731625493765e-3 + z * 2.443315711809948e-5))
    odd = (quadrant & 1) == 1
    cos_abs = jnp.where(odd, s, c)
    sin_abs = jnp.where(odd, c, s)
    cos = jnp.where(((quadrant + 1) & 2) == 2, -cos_abs, cos_abs)
    sin = jnp.where((quadrant & 2) == 2, -sin_abs, sin_abs)
    return cos, sin


def repeat(count, body):
    if count <= 8:
        for i in range(count):
            body(i)
    else:
        lax.fori_loop(0, count, lambda i, carry: (body(i), carry)[1], 0)


def multiple(value, of):
    return value if isinstance(value, int) else pl.multiple_of(value, of)


def lane_gather(values, at):
    dims = lax.GatherDimensionNumbers(
        offset_dims=(),
        collapsed_slice_dims=(1,),
        start_index_map=(1,),
        operand_batching_dims=(0,),
        start_indices_batching_dims=(0,),
    )
    return lax.gather(values, at[..., None], dims, (1, 1), mode=lax.GatherScatterMode.PROMISE_IN_BOUNDS)


def iota(shape, dim):
    return lax.broadcasted_iota(jnp.int32, shape, dim)


def shift(values, by):
    return lax.shift_right_logical(values, jnp.full_like(values, by))


STEP, FIRST = (2, 4, 8, 8), (1, 2, 4, 0)
RESIDUES = (0, 4, 2, 6, 1, 5, 3, 7)


def class_order():
    row, column = iota((LANES, LANES), 0), iota((LANES, LANES), 1)
    bin_of, first = jnp.full_like(row, 0), 0
    for step, start in zip(STEP, FIRST):
        bin_of = jnp.where(row >= first, step * (row - first) + start, bin_of)
        first += LANES // step
    return jnp.where(bin_of == column, 1.0, 0.0).astype(BF16)


def quarter_turns(value, count):
    odd = (count & 1) == 1
    cos, sin = jnp.where(odd, value[1], value[0]), jnp.where(odd, value[0], value[1])
    return jnp.where(((count + 1) & 2) == 2, -cos, cos), jnp.where((count & 2) == 2, -sin, sin)


def times(one, other):
    return one[0] * other[0] - one[1] * other[1], one[1] * other[0] + one[0] * other[1]


def dedisperse_kernel(
    trials_each, dm_hbm, cd_hbm, sp_hbm, send_ref, keep_ref, dm_ref, cd_ref, sp, ph, turned, y0, y1, xs, sems
):
    channels, bins = sp.shape[1:]
    samples = 2 * bins
    half = LANES // 2
    tiles = bins // LANES
    spread = bins // (8 * half)
    chunks = 8 * spread
    chan = lax.axis_index("chan")
    block = chan * lax.axis_size("bin") + lax.axis_index("bin")
    fetches = [
        pltpu.make_async_copy(source, target, sems.at[n])
        for n, (source, target) in enumerate(((cd_hbm, cd_ref), (sp_hbm, sp), (dm_hbm, dm_ref)))
    ]
    for fetch in fetches:
        fetch.start()
    order = class_order()
    edge = jnp.zeros((send_ref.shape[0], EDGE), BF16)
    for ref in (send_ref, keep_ref):
        ref[:, :EDGE] = edge
        ref[:, bins + EDGE :] = edge

    fetches[0].wait()
    if channels >= LANES:
        lines = [cd_ref[pl.ds(block * (channels // LANES) + k, 1), :] for k in range(channels // LANES)]
    else:
        first = block * channels
        line = cd_ref[pl.ds(first // LANES, 1), :]
        lines = [pltpu.roll(jnp.broadcast_to(line, (SUB, LANES)), (LANES - first % LANES) % LANES, 1)[:1]]

    def to_column(lines):
        return jnp.concatenate([jnp.broadcast_to(line, (LANES, LANES)).T for line in lines], axis=0)[:channels]

    cd = to_column(lines)
    own_turns = [sincos(line & (samples - 1), samples) for line in lines]
    column = iota(cd.shape, 1)
    start = 8 * (column & (half - 1)) * cd - jnp.where(column >= half, samples // 4, 0)
    turns = {1: tuple(to_column([turn[n] for turn in own_turns]) for n in range(2))}
    turns[2] = times(turns[1], turns[1])
    turns[4] = times(turns[2], turns[2])
    bases = [{0: sincos(start & (samples - 1), samples)}]
    for h in range(1, spread):
        if 8 * half * h * 4 == samples:
            bases.append({0: quarter_turns(bases[0][0], cd)})
        else:
            bases.append({0: sincos((start + 8 * half * h * cd) & (samples - 1), samples)})

    def make_phases(residue):
        for h in range(spread):
            if residue:
                by = residue & -residue
                bases[h][residue] = times(bases[h][residue - by], turns[by])
            value = bases[h][residue][0]
            if h == 0 and residue == 0:
                value = jnp.where(column == half, (1 - 2 * (cd & 1)).astype(F32), value)
            at = (RESIDUES.index(residue) * spread + h) * LANES
            ph[:, at : at + LANES] = value.astype(BF16)

    for residue in (0, 4, 2, 6, 1, 5, 3, 7):
        make_phases(residue)
    fetches[1].wait()
    fetches[2].wait()
    lane = iota((16, LANES), 1)
    trial = ((lane // (2 * trials_each)) ^ chan) * trials_each + (lane & (trials_each - 1))
    dm = jnp.concatenate([dm_ref[...], dm_ref[...]], axis=1)
    dm = jnp.take_along_axis(jnp.broadcast_to(dm, (16, LANES)), trial, axis=1)
    imag = (lane & trials_each).astype(jnp.int16) != 0
    row = iota((16, LANES), 0)
    own_half = jnp.where((lane & trials_each) != 0, half, 0).astype(jnp.int16)
    other_half = own_half ^ half
    zero, one = jnp.zeros((16, LANES), BF16), jnp.ones((16, LANES), BF16)
    running = {}
    starts = [sum(bins // s for s in STEP[:k]) for k in range(4)]

    def turn_tile(t):
        columns = pl.ds(multiple(t * LANES, LANES), LANES)
        for part in range(2):
            rows = lax.dot_general(order, sp[part, :, columns], (((1,), (1,)), ((), ())), preferred_element_type=F32)
            rows = rows.astype(BF16)
            first = 0
            for k in range(4):
                size = LANES // STEP[k]
                turned[part, pl.ds(multiple(starts[k] + t * size, 16), size), :] = rows[first : first + size]
                first += size

    def multiply(k, b, size, y):
        columns = (chunks >> k) * LANES
        rows = pl.ds(multiple(starts[k] + b * size, 16), size)
        for part in range(2):
            for at in range(0, columns, 256):
                y[part, :size, at : at + 256] = jnp.dot(
                    turned[part, rows, :], ph[:, at : at + 256], preferred_element_type=F32
                ).astype(BF16)

    def pick(k, b, size, y):
        each = LANES // STEP[k]
        tile_first = sum(LANES // s for s in STEP[:k])

        begin = ((STEP[k] * row + FIRST[k]) * dm).astype(jnp.int16)
        more = (16 * STEP[k] * dm).astype(jnp.int16)

        def group(i, product=None):
            base = b * size + i * 16
            if product is None:
                product = ((STEP[k] * (base + row) + FIRST[k]) * dm).astype(jnp.int16)
            unused = 16 - samples.bit_length() + 1
            signed = lax.shift_left(product, jnp.full_like(product, unused))
            signed = lax.shift_right_arithmetic(signed, jnp.full_like(signed, unused))
            near = jnp.abs(signed)
            key = near & (bins - 1 - 8 * (half - 1))
            at_re = (shift(near, 3) & (half - 1)) ^ jnp.where(signed == -bins, other_half, own_half)
            at_im = at_re ^ half
            got = []
            for part, at in ((0, at_re), (1, at_im)):
                value = None
                for j in range(chunks >> k):
                    lanes = slice(j * LANES, (j + 1) * LANES)
                    new = lane_gather(y[part, pl.ds(multiple(i * 16, 16), 16), lanes], at)
                    this = RESIDUES[j // spread] + 8 * half * (j % spread)
                    value = new if value is None else jnp.where(key == this, new, value)
                got.append(value)
            sign = jnp.where(signed < 0, -one, one)
            sign = jnp.where((signed & (bins - 1)) == 0, zero, sign)
            total = got[0] * jnp.where(imag, -sign, one) + got[1] * jnp.where(imag, one, sign)
            at = (base // each) * LANES + tile_first + base % each
            xs[pl.ds(multiple(at, 16), 16), :] = total
            return product

        if isinstance(b, int) and size // 16 <= 8:
            product = running.get(k, begin)
            for i in range(size // 16):
                group(i, product)
                product = product + more
            running[k] = product
            return
        repeat(size // 16, group)

    wide = 2 * trials_each

    def finish(t):
        rows = xs[pl.ds(multiple(t * LANES, LANES), LANES), :]
        out = lax.dot_general(rows, order, (((0,), (0,)), ((), ())), preferred_element_type=F32).astype(BF16)
        columns = pl.ds(multiple(EDGE + t * LANES, LANES), LANES)
        for k in range(LANES // wide):
            ref = (keep_ref, send_ref)[k % 2]
            ref[(k // 2) * wide : (k // 2 + 1) * wide, columns] = out[k * wide : (k + 1) * wide]

    size = y0.shape[1]
    sizes = [min(size, bins // s) for s in STEP]
    counts = [bins // s // own for s, own in zip(STEP, sizes)]
    if tiles <= 8:
        work = [(k, b, sizes[k]) for k in (0, 1, 2, 3) for b in range(counts[k])]
        buffers = (y0, y1)
        for t in range(tiles):
            turn_tile(t)
        multiply(*work[0], y0)
        for n, item in enumerate(work):
            if n + 1 < len(work):
                multiply(*work[n + 1], buffers[(n + 1) % 2])
            pick(*item, buffers[n % 2])
        for t in range(tiles):
            finish(t)
    else:
        repeat(tiles, turn_tile)
        for k in range(4):

            def whole_block(b, carry, k=k):
                multiply(k, b, sizes[k], y0)
                pick(k, b, sizes[k], y0)
                return carry

            lax.fori_loop(0, counts[k], whole_block, 0)
        repeat(tiles, finish)


def dedisperse(spectra, dm_trials, chan_delay, trials_each):
    _, channels, bins = spectra.shape
    size = 128
    rows = LANES // 2
    dm = dm_trials.reshape(1, -1)
    delays = chan_delay.reshape(-1, LANES)
    out = pltpu.VMEM((rows, bins + 2 * EDGE), BF16)
    room = 12 * rows * (bins + 2 * EDGE) * 2
    return pl.pallas_call(
        functools.partial(dedisperse_kernel, trials_each),
        in_specs=[pl.BlockSpec(memory_space=pltpu.HBM)] * 3,
        out_specs=[pl.BlockSpec(memory_space=pltpu.VMEM)] * 2,
        out_shape=[out] * 2,
        scratch_shapes=[
            pltpu.VMEM(dm.shape, jnp.int32),
            pltpu.VMEM(delays.shape, jnp.int32),
            pltpu.VMEM(spectra.shape, BF16),
            pltpu.VMEM((channels, 2 * bins), BF16),
            pltpu.VMEM((2, bins, channels), BF16),
            pltpu.VMEM((2, size, 2 * bins), BF16),
            pltpu.VMEM((2, size, 2 * bins), BF16),
            pltpu.VMEM((bins, LANES), BF16),
            pltpu.SemaphoreType.DMA((3,)),
        ],
        compiler_params=pltpu.CompilerParams(vmem_limit_bytes=min(62 * 2**20, 64 * 2**20 - room)),
        name="dedisperse",
    )(dm, delays, spectra)


def pick_kernel(bank_ref, ids_ref, out_ref):
    bank, taps = bank_ref.shape[1:]
    count = ids_ref.shape[1]
    rows = lax.broadcasted_iota(jnp.int32, (bank, count), 0)
    one_hot = jnp.where(rows == ids_ref[...], 1.0, 0.0).astype(BF16)
    at = lax.broadcasted_iota(jnp.int32, (taps, taps), 0)
    to = lax.broadcasted_iota(jnp.int32, (taps, taps), 1)
    flip = jnp.where(at == (to ^ 15), 1.0, 0.0).astype(BF16)
    chosen = []
    for part in range(2):
        taken = lax.dot_general(one_hot, bank_ref[part], (((0,), (0,)), ((), ())), preferred_element_type=F32)
        chosen.append(jnp.dot(taken.astype(BF16), flip, preferred_element_type=F32))
    re, im = chosen
    out_ref[:count, :taps] = re.astype(BF16)
    out_ref[:count, taps:] = (-im).astype(BF16)
    out_ref[count:, :taps] = im.astype(BF16)
    out_ref[count:, taps:] = re.astype(BF16)


def pick_templates(template_bank, template_ids):
    _, bank, taps = template_bank.shape
    count = template_ids.shape[0]
    return pl.pallas_call(
        pick_kernel,
        out_shape=pltpu.VMEM((2 * count, 2 * taps), BF16),
        cost_estimate=pl.CostEstimate(flops=4 * count * bank * taps, bytes_accessed=2**20, transcendentals=0),
        name="pick_templates",
    )(template_bank, template_ids.reshape(1, -1))


def search_kernel(scale, near_ref, far_ref, templates_ref, out_hbm, signal, out, sems):
    trials, count, bins = out.shape
    width = near_ref.shape[1]
    taps = templates_ref.shape[1] // 2
    total = near_ref[...].astype(F32) + far_ref[...].astype(F32)
    signal[...] = (total * scale).astype(BF16).astype(F32)
    each = trials // sems.shape[0]
    ahead = iota((16, LANES), 1) + 15 - iota((16, LANES), 0)
    ats = [(ahead + 16 * e & (LANES - 1)).astype(jnp.int16) for e in range(LANES // 16)]
    stays = [(ahead + 16 * e).astype(jnp.int16) < LANES for e in range(LANES // 16)]

    def fill(trial, part):
        line = signal[pl.ds(part * trials + trial, 1), :]
        line = jnp.broadcast_to(line, (16, width)).astype(BF16)
        pieces = [line[:, v * LANES : (v + 1) * LANES] for v in range(width // LANES)]
        moved = []
        for e in range(LANES // 16):
            turned = [lane_gather(piece, ats[e]) for piece in pieces]
            moved.append([jnp.where(stays[e], turned[v], turned[v + 1]) for v in range(len(turned) - 1)])
        rows = []
        for h in range(taps // LANES):
            for e in range(LANES // 16):
                rows.append(jnp.concatenate([moved[e][h + v] for v in range(bins // LANES)], axis=1))
        return jnp.concatenate(rows, axis=0)

    copies = []
    for trial in range(trials):
        response = sum(
            jnp.dot(templates_ref[:, part * taps : (part + 1) * taps], fill(trial, part), preferred_element_type=F32)
            for part in range(2)
        )
        re, im = response[:count], response[count:]
        out[trial] = (re * re + im * im).astype(BF16)
        if trial % each == each - 1:
            here = pl.ds(trial + 1 - each, each)
            copies.append(pltpu.make_async_copy(out.at[here], out_hbm.at[here], sems.at[trial // each]))
            copies[-1].start()
    for copy in copies:
        copy.wait()


def search(near, far, templates, scale, bins):
    rows, width = near.shape
    trials = rows // 2
    taps = templates.shape[1] // 2
    count = templates.shape[0] // 2
    in_vmem = pl.BlockSpec(memory_space=pltpu.VMEM)
    return pl.pallas_call(
        functools.partial(search_kernel, scale),
        in_specs=[in_vmem] * 3,
        out_specs=pl.BlockSpec(memory_space=pltpu.HBM),
        out_shape=jax.ShapeDtypeStruct((trials, count, bins), BF16),
        scratch_shapes=[
            pltpu.VMEM((rows, width), F32),
            pltpu.VMEM((trials, count, bins), BF16),
            pltpu.SemaphoreType.DMA((min(trials, 4),)),
        ],
        compiler_params=pltpu.CompilerParams(vmem_limit_bytes=32 * 2**20),
        name="search",
    )(near, far, templates)


def swap(cells, owner_bit, span_bit):
    owners, spans = lax.axis_size("chan"), lax.axis_size("bin")
    pairs = [(i, i ^ (span_bit * owners + owner_bit)) for i in range(owners * spans)]
    return lax.ppermute(cells, ("bin", "chan"), pairs)


def add(*cells):
    return sum(cell.astype(F32) for cell in cells).astype(BF16)


def local(spectra, dm_trials, chan_delay, template_bank, template_ids):
    owners, spans = lax.axis_size("chan"), lax.axis_size("bin")
    bins = spectra.shape[2]
    own_bins = bins // spans
    trials_each = dm_trials.shape[0] // owners
    scale = 1.0 / math.sqrt(chan_delay.shape[0])
    wide = 2 * trials_each
    place = lax.axis_index("bin")
    templates = pick_templates(template_bank, template_ids)
    send, keep = dedisperse(spectra, dm_trials, chan_delay, trials_each)
    distance = 1
    while 2 * distance < owners:
        total = add(keep, swap(send, distance, 0)).reshape(-1, 2, wide, keep.shape[1])
        keep, send = total[:, 0].reshape(-1, keep.shape[1]), total[:, 1].reshape(-1, keep.shape[1])
        distance *= 2
    reach = (spans - 1) * own_bins + 2 * EDGE
    odd = (place & 1) != 0

    def by_parity(cells):
        low, high = cells[:, :reach], cells[:, own_bins : own_bins + reach]
        return jnp.where(odd, high, low), jnp.where(odd, low, high)

    keep, keep_far = by_parity(keep)
    send, send_far = by_parity(send)
    send_far, keep_far, send = lax.optimization_barrier((send_far, keep_far, send))
    keep = add(keep, swap(send_far, distance, 1), swap(keep_far, 0, 1), swap(send, distance, 0))
    keep, templates = lax.optimization_barrier((keep, templates))
    part = spans // 2
    while True:
        width = (part // 2 - 1) * 2 * own_bins + own_bins + 2 * EDGE
        upper = (place & part) != 0
        left, right = keep[:, :width], keep[:, part * own_bins : part * own_bins + width]
        keep, send = jnp.where(upper, right, left), jnp.where(upper, left, right)
        got = swap(send, 0, part)
        if part == 2:
            return search(keep, got, templates, scale, own_bins)
        keep = add(keep, got)
        part //= 2


def solution(mesh):
    in_specs = (P(None, ("beam", "chan", "bin"), None), P(), P(), P(), P())
    out_specs = P(("beam", "chan"), None, "bin")
    return jax.shard_map(local, mesh=mesh, in_specs=in_specs, out_specs=out_specs, check_vma=False)
```

```python
import functools
import math

import jax
import jax.numpy as jnp
from jax import lax
from jax.experimental import pallas as pl
from jax.experimental.pallas import tpu as pltpu
from jax.sharding import PartitionSpec as P

EDGE = 128
LANES = 128
SUB = 8
F32 = jnp.float32
BF16 = jnp.bfloat16


def sincos(turn, samples):
    quarter = samples // 4
    quadrant = (turn + quarter // 2) // quarter if quarter & (quarter - 1) else lax.shift_right_logical(
        turn + quarter // 2, jnp.full_like(turn, quarter.bit_length() - 1)
    )
    y = (turn - quadrant * quarter).astype(F32) * (2.0 * math.pi / samples)
    z = y * y
    s = y + y * z * (-1.6666654611e-1 + z * (8.3321608736e-3 - z * 1.9515295891e-4))
    c = 1.0 - 0.5 * z + z * z * (4.166664568298827e-2 + z * (-1.388731625493765e-3 + z * 2.443315711809948e-5))
    odd = (quadrant & 1) == 1
    cos_abs = jnp.where(odd, s, c)
    sin_abs = jnp.where(odd, c, s)
    cos = jnp.where(((quadrant + 1) & 2) == 2, -cos_abs, cos_abs)
    sin = jnp.where((quadrant & 2) == 2, -sin_abs, sin_abs)
    return cos, sin


def repeat(count, body):
    if count <= 8:
        for i in range(count):
            body(i)
    else:
        lax.fori_loop(0, count, lambda i, carry: (body(i), carry)[1], 0)


def multiple(value, of):
    return value if isinstance(value, int) else pl.multiple_of(value, of)


def lane_gather(values, at):
    dims = lax.GatherDimensionNumbers(
        offset_dims=(),
        collapsed_slice_dims=(1,),
        start_index_map=(1,),
        operand_batching_dims=(0,),
        start_indices_batching_dims=(0,),
    )
    return lax.gather(values, at[..., None], dims, (1, 1), mode=lax.GatherScatterMode.PROMISE_IN_BOUNDS)


def iota(shape, dim):
    return lax.broadcasted_iota(jnp.int32, shape, dim)


def shift(values, by):
    return lax.shift_right_logical(values, jnp.full_like(values, by))


STEP, FIRST = (2, 4, 8, 8), (1, 2, 4, 0)
RESIDUES = (0, 4, 2, 6, 1, 5, 3, 7)


def class_order():
    row, column = iota((LANES, LANES), 0), iota((LANES, LANES), 1)
    bin_of, first = jnp.full_like(row, 0), 0
    for step, start in zip(STEP, FIRST):
        bin_of = jnp.where(row >= first, step * (row - first) + start, bin_of)
        first += LANES // step
    return jnp.where(bin_of == column, 1.0, 0.0).astype(BF16)


def quarter_turns(value, count):
    odd = (count & 1) == 1
    cos, sin = jnp.where(odd, value[1], value[0]), jnp.where(odd, value[0], value[1])
    return jnp.where(((count + 1) & 2) == 2, -cos, cos), jnp.where((count & 2) == 2, -sin, sin)


def times(one, other):
    return one[0] * other[0] - one[1] * other[1], one[1] * other[0] + one[0] * other[1]


def dedisperse_kernel(
    trials_each, dm_hbm, cd_hbm, sp_hbm, send_ref, keep_ref, dm_ref, cd_ref, sp, ph, turned, y0, y1, xs, sems
):
    channels, bins = sp.shape[1:]
    samples = 2 * bins
    half = LANES // 2
    tiles = bins // LANES
    spread = bins // (8 * half)
    chunks = 8 * spread
    chan = lax.axis_index("chan")
    block = chan * lax.axis_size("bin") + lax.axis_index("bin")
    fetches = [
        pltpu.make_async_copy(source, target, sems.at[n])
        for n, (source, target) in enumerate(((cd_hbm, cd_ref), (sp_hbm, sp), (dm_hbm, dm_ref)))
    ]
    for fetch in fetches:
        fetch.start()
    order = class_order()
    edge = jnp.zeros((send_ref.shape[0], EDGE), BF16)
    for ref in (send_ref, keep_ref):
        ref[:, :EDGE] = edge
        ref[:, bins + EDGE :] = edge

    fetches[0].wait()
    if channels >= LANES:
        lines = [cd_ref[pl.ds(block * (channels // LANES) + k, 1), :] for k in range(channels // LANES)]
    else:
        first = block * channels
        line = cd_ref[pl.ds(first // LANES, 1), :]
        lines = [pltpu.roll(jnp.broadcast_to(line, (SUB, LANES)), (LANES - first % LANES) % LANES, 1)[:1]]

    def to_column(lines):
        return jnp.concatenate([jnp.broadcast_to(line, (LANES, LANES)).T for line in lines], axis=0)[:channels]

    cd = to_column(lines)
    own_turns = [sincos(line & (samples - 1), samples) for line in lines]
    column = iota(cd.shape, 1)
    start = 8 * (column & (half - 1)) * cd - jnp.where(column >= half, samples // 4, 0)
    turns = {1: tuple(to_column([turn[n] for turn in own_turns]) for n in range(2))}
    turns[2] = times(turns[1], turns[1])
    turns[4] = times(turns[2], turns[2])
    bases = [{0: sincos(start & (samples - 1), samples)}]
    for h in range(1, spread):
        if 8 * half * h * 4 == samples:
            bases.append({0: quarter_turns(bases[0][0], cd)})
        else:
            bases.append({0: sincos((start + 8 * half * h * cd) & (samples - 1), samples)})

    def make_phases(residue):
        for h in range(spread):
            if residue:
                by = residue & -residue
                bases[h][residue] = times(bases[h][residue - by], turns[by])
            value = bases[h][residue][0]
            if h == 0 and residue == 0:
                value = jnp.where(column == half, (1 - 2 * (cd & 1)).astype(F32), value)
            at = (RESIDUES.index(residue) * spread + h) * LANES
            ph[:, at : at + LANES] = value.astype(BF16)

    for residue in (0, 4, 2, 6, 1, 5, 3, 7):
        make_phases(residue)
    fetches[1].wait()
    fetches[2].wait()
    lane = iota((16, LANES), 1)
    trial = ((lane // (2 * trials_each)) ^ chan) * trials_each + (lane & (trials_each - 1))
    dm = jnp.concatenate([dm_ref[...], dm_ref[...]], axis=1)
    dm = jnp.take_along_axis(jnp.broadcast_to(dm, (16, LANES)), trial, axis=1)
    imag = (lane & trials_each).astype(jnp.int16) != 0
    row = iota((16, LANES), 0)
    own_half = jnp.where((lane & trials_each) != 0, half, 0).astype(jnp.int16)
    other_half = own_half ^ half
    zero, one = jnp.zeros((16, LANES), BF16), jnp.ones((16, LANES), BF16)
    running = {}
    starts = [sum(bins // s for s in STEP[:k]) for k in range(4)]

    def turn_tile(t):
        columns = pl.ds(multiple(t * LANES, LANES), LANES)
        for part in range(2):
            rows = lax.dot_general(order, sp[part, :, columns], (((1,), (1,)), ((), ())), preferred_element_type=F32)
            rows = rows.astype(BF16)
            first = 0
            for k in range(4):
                size = LANES // STEP[k]
                turned[part, pl.ds(multiple(starts[k] + t * size, 16), size), :] = rows[first : first + size]
                first += size

    def multiply(k, b, size, y):
        columns = (chunks >> k) * LANES
        rows = pl.ds(multiple(starts[k] + b * size, 16), size)
        for part in range(2):
            for at in range(0, columns, 256):
                y[part, :size, at : at + 256] = jnp.dot(
                    turned[part, rows, :], ph[:, at : at + 256], preferred_element_type=F32
                ).astype(BF16)

    def pick(k, b, size, y):
        each = LANES // STEP[k]
        tile_first = sum(LANES // s for s in STEP[:k])

        begin = ((STEP[k] * row + FIRST[k]) * dm).astype(jnp.int16)
        more = (16 * STEP[k] * dm).astype(jnp.int16)

        def group(i, product=None):
            base = b * size + i * 16
            if product is None:
                product = ((STEP[k] * (base + row) + FIRST[k]) * dm).astype(jnp.int16)
            unused = 16 - samples.bit_length() + 1
            signed = lax.shift_left(product, jnp.full_like(product, unused))
            signed = lax.shift_right_arithmetic(signed, jnp.full_like(signed, unused))
            near = jnp.abs(signed)
            key = near & (bins - 1 - 8 * (half - 1))
            at_re = (shift(near, 3) & (half - 1)) ^ jnp.where(signed == -bins, other_half, own_half)
            at_im = at_re ^ half
            got = []
            for part, at in ((0, at_re), (1, at_im)):
                value = None
                for j in range(chunks >> k):
                    lanes = slice(j * LANES, (j + 1) * LANES)
                    new = lane_gather(y[part, pl.ds(multiple(i * 16, 16), 16), lanes], at)
                    this = RESIDUES[j // spread] + 8 * half * (j % spread)
                    value = new if value is None else jnp.where(key == this, new, value)
                got.append(value)
            sign = jnp.where(signed < 0, -one, one)
            sign = jnp.where((signed & (bins - 1)) == 0, zero, sign)
            total = got[0] * jnp.where(imag, -sign, one) + got[1] * jnp.where(imag, one, sign)
            at = (base // each) * LANES + tile_first + base % each
            xs[pl.ds(multiple(at, 16), 16), :] = total
            return product

        if isinstance(b, int) and size // 16 <= 8:
            product = running.get(k, begin)
            for i in range(size // 16):
                group(i, product)
                product = product + more
            running[k] = product
            return
        repeat(size // 16, group)

    wide = 2 * trials_each

    def finish(t):
        rows = xs[pl.ds(multiple(t * LANES, LANES), LANES), :]
        out = lax.dot_general(rows, order, (((0,), (0,)), ((), ())), preferred_element_type=F32).astype(BF16)
        columns = pl.ds(multiple(EDGE + t * LANES, LANES), LANES)
        for k in range(LANES // wide):
            ref = (keep_ref, send_ref)[k % 2]
            ref[(k // 2) * wide : (k // 2 + 1) * wide, columns] = out[k * wide : (k + 1) * wide]

    size = y0.shape[1]
    sizes = [min(size, bins // s) for s in STEP]
    counts = [bins // s // own for s, own in zip(STEP, sizes)]
    if tiles <= 8:
        work = [(k, b, sizes[k]) for k in (1, 0, 2, 3) for b in range(counts[k])]
        buffers = (y0, y1)
        for t in range(tiles):
            turn_tile(t)
        multiply(*work[0], y0)
        for n, item in enumerate(work):
            if n + 1 < len(work):
                multiply(*work[n + 1], buffers[(n + 1) % 2])
            pick(*item, buffers[n % 2])
        for t in range(tiles):
            finish(t)
    else:
        repeat(tiles, turn_tile)
        for k in range(4):

            def whole_block(b, carry, k=k):
                multiply(k, b, sizes[k], y0)
                pick(k, b, sizes[k], y0)
                return carry

            lax.fori_loop(0, counts[k], whole_block, 0)
        repeat(tiles, finish)


def dedisperse(spectra, dm_trials, chan_delay, trials_each):
    _, channels, bins = spectra.shape
    size = 128
    rows = LANES // 2
    dm = dm_trials.reshape(1, -1)
    delays = chan_delay.reshape(-1, LANES)
    out = pltpu.VMEM((rows, bins + 2 * EDGE), BF16)
    room = 12 * rows * (bins + 2 * EDGE) * 2
    return pl.pallas_call(
        functools.partial(dedisperse_kernel, trials_each),
        in_specs=[pl.BlockSpec(memory_space=pltpu.HBM)] * 3,
        out_specs=[pl.BlockSpec(memory_space=pltpu.VMEM)] * 2,
        out_shape=[out] * 2,
        scratch_shapes=[
            pltpu.VMEM(dm.shape, jnp.int32),
            pltpu.VMEM(delays.shape, jnp.int32),
            pltpu.VMEM(spectra.shape, BF16),
            pltpu.VMEM((channels, 2 * bins), BF16),
            pltpu.VMEM((2, bins, channels), BF16),
            pltpu.VMEM((2, size, 2 * bins), BF16),
            pltpu.VMEM((2, size, 2 * bins), BF16),
            pltpu.VMEM((bins, LANES), BF16),
            pltpu.SemaphoreType.DMA((3,)),
        ],
        compiler_params=pltpu.CompilerParams(vmem_limit_bytes=min(62 * 2**20, 64 * 2**20 - room)),
        name="dedisperse",
    )(dm, delays, spectra)


def pick_kernel(bank_ref, ids_ref, out_ref):
    bank, taps = bank_ref.shape[1:]
    count = ids_ref.shape[1]
    rows = lax.broadcasted_iota(jnp.int32, (bank, count), 0)
    one_hot = jnp.where(rows == ids_ref[...], 1.0, 0.0).astype(BF16)
    at = lax.broadcasted_iota(jnp.int32, (taps, taps), 0)
    to = lax.broadcasted_iota(jnp.int32, (taps, taps), 1)
    flip = jnp.where(at == (to ^ 15), 1.0, 0.0).astype(BF16)
    chosen = []
    for part in range(2):
        taken = lax.dot_general(one_hot, bank_ref[part], (((0,), (0,)), ((), ())), preferred_element_type=F32)
        chosen.append(jnp.dot(taken.astype(BF16), flip, preferred_element_type=F32))
    re, im = chosen
    out_ref[:count, :taps] = re.astype(BF16)
    out_ref[:count, taps:] = (-im).astype(BF16)
    out_ref[count:, :taps] = im.astype(BF16)
    out_ref[count:, taps:] = re.astype(BF16)


def pick_templates(template_bank, template_ids):
    _, bank, taps = template_bank.shape
    count = template_ids.shape[0]
    return pl.pallas_call(
        pick_kernel,
        out_shape=pltpu.VMEM((2 * count, 2 * taps), BF16),
        cost_estimate=pl.CostEstimate(flops=4 * count * bank * taps, bytes_accessed=2**20, transcendentals=0),
        name="pick_templates",
    )(template_bank, template_ids.reshape(1, -1))


def search_kernel(scale, near_ref, far_ref, templates_ref, out_hbm, signal, out, sems):
    trials, count, bins = out.shape
    width = near_ref.shape[1]
    taps = templates_ref.shape[1] // 2
    total = near_ref[...].astype(F32) + far_ref[...].astype(F32)
    signal[...] = (total * scale).astype(BF16).astype(F32)
    each = trials // sems.shape[0]
    ahead = iota((16, LANES), 1) + 15 - iota((16, LANES), 0)
    ats = [(ahead + 16 * e & (LANES - 1)).astype(jnp.int16) for e in range(LANES // 16)]
    stays = [(ahead + 16 * e).astype(jnp.int16) < LANES for e in range(LANES // 16)]

    def fill(trial, part):
        line = signal[pl.ds(part * trials + trial, 1), :]
        line = jnp.broadcast_to(line, (16, width)).astype(BF16)
        pieces = [line[:, v * LANES : (v + 1) * LANES] for v in range(width // LANES)]
        moved = []
        for e in range(LANES // 16):
            turned = [lane_gather(piece, ats[e]) for piece in pieces]
            moved.append([jnp.where(stays[e], turned[v], turned[v + 1]) for v in range(len(turned) - 1)])
        rows = []
        for h in range(taps // LANES):
            for e in range(LANES // 16):
                rows.append(jnp.concatenate([moved[e][h + v] for v in range(bins // LANES)], axis=1))
        return jnp.concatenate(rows, axis=0)

    copies = []
    for trial in range(trials):
        response = sum(
            jnp.dot(templates_ref[:, part * taps : (part + 1) * taps], fill(trial, part), preferred_element_type=F32)
            for part in range(2)
        )
        re, im = response[:count], response[count:]
        out[trial] = (re * re + im * im).astype(BF16)
        if trial % each == each - 1:
            here = pl.ds(trial + 1 - each, each)
            copies.append(pltpu.make_async_copy(out.at[here], out_hbm.at[here], sems.at[trial // each]))
            copies[-1].start()
    for copy in copies:
        copy.wait()


def search(near, far, templates, scale, bins):
    rows, width = near.shape
    trials = rows // 2
    taps = templates.shape[1] // 2
    count = templates.shape[0] // 2
    in_vmem = pl.BlockSpec(memory_space=pltpu.VMEM)
    return pl.pallas_call(
        functools.partial(search_kernel, scale),
        in_specs=[in_vmem] * 3,
        out_specs=pl.BlockSpec(memory_space=pltpu.HBM),
        out_shape=jax.ShapeDtypeStruct((trials, count, bins), BF16),
        scratch_shapes=[
            pltpu.VMEM((rows, width), F32),
            pltpu.VMEM((trials, count, bins), BF16),
            pltpu.SemaphoreType.DMA((min(trials, 4),)),
        ],
        compiler_params=pltpu.CompilerParams(vmem_limit_bytes=32 * 2**20),
        name="search",
    )(near, far, templates)


def swap(cells, owner_bit, span_bit):
    owners, spans = lax.axis_size("chan"), lax.axis_size("bin")
    pairs = [(i, i ^ (span_bit * owners + owner_bit)) for i in range(owners * spans)]
    return lax.ppermute(cells, ("bin", "chan"), pairs)


def add(*cells):
    return sum(cell.astype(F32) for cell in cells).astype(BF16)


def local(spectra, dm_trials, chan_delay, template_bank, template_ids):
    owners, spans = lax.axis_size("chan"), lax.axis_size("bin")
    bins = spectra.shape[2]
    own_bins = bins // spans
    trials_each = dm_trials.shape[0] // owners
    scale = 1.0 / math.sqrt(chan_delay.shape[0])
    wide = 2 * trials_each
    place = lax.axis_index("bin")
    templates = pick_templates(template_bank, template_ids)
    send, keep = dedisperse(spectra, dm_trials, chan_delay, trials_each)
    distance = 1
    while 2 * distance < owners:
        total = add(keep, swap(send, distance, 0)).reshape(-1, 2, wide, keep.shape[1])
        keep, send = total[:, 0].reshape(-1, keep.shape[1]), total[:, 1].reshape(-1, keep.shape[1])
        distance *= 2
    reach = (spans - 1) * own_bins + 2 * EDGE
    odd = (place & 1) != 0

    def by_parity(cells):
        low, high = cells[:, :reach], cells[:, own_bins : own_bins + reach]
        return jnp.where(odd, high, low), jnp.where(odd, low, high)

    keep, keep_far = by_parity(keep)
    send, send_far = by_parity(send)
    send_far, keep_far, send = lax.optimization_barrier((send_far, keep_far, send))
    keep = add(keep, swap(send_far, distance, 1), swap(keep_far, 0, 1), swap(send, distance, 0))
    part = spans // 2
    while True:
        width = (part // 2 - 1) * 2 * own_bins + own_bins + 2 * EDGE
        upper = (place & part) != 0
        left, right = keep[:, :width], keep[:, part * own_bins : part * own_bins + width]
        keep, send = jnp.where(upper, right, left), jnp.where(upper, left, right)
        got = swap(send, 0, part)
        if part == 2:
            return search(keep, got, templates, scale, own_bins)
        keep = add(keep, got)
        part //= 2


def solution(mesh):
    in_specs = (P(None, ("beam", "chan", "bin"), None), P(), P(), P(), P())
    out_specs = P(("beam", "chan"), None, "bin")
    return jax.shard_map(local, mesh=mesh, in_specs=in_specs, out_specs=out_specs, check_vma=False)
```
